512 devices in a mesh: seq: 32 (over z_hi, y, core), chan: 16 (over x, z_lo).
Axes of the slice: x: 4, y: 8, z: 8 (z_hi: 2, z_lo: 4; z = z_hi * 4 + z_lo), core: 2. Of those that a mesh axis runs over, the one named last changes fastest.
Arguments:
- query: bfloat16 [131072, 256], P(('seq', 'chan')), may hold values from -6 to 6
- keys: bfloat16 [131072, 256], P(('seq', 'chan')), may hold values from -6 to 6
- values: bfloat16 [131072, 256], P(('seq', 'chan')), may hold values from -6 to 6
- decay: float32 [32, 16], P('chan'), may hold values from 3.8146973e-06 to 0.03
- residue: float32 [32, 16], P('chan'), may hold values from -2.5 to 2.5
- skip: float32 [256], P('chan'), may hold values from 0.5 to 1.5
Outputs:
- gated: bfloat16 [131072, 256], P(('seq', 'chan'))
The draws below stay inside these ranges and needn't reach their ends.
All inputs are finite; a program needn't handle non-finite values.
Results may differ from the reference program's by a relative error of at most 0.0085.
Values may be sent and summed in bfloat16 or wider, within the bound.
No kernel may reach another device: no remote copies, remote signals or barrier semaphores. Data moves between devices by JAX's collectives and lax.ppermute only.
A program may use at most 128 MiB of HBM per device.

```python
import math
import jax
import jax.numpy as jnp
from jax import lax

CH = 256
GSZ = 8
ORDER = 16
LEN = 131072
GROUPS = 32


def levels(own_key, shape, cuts, smallest, top_value):
    level, own = 1.0, jax.random.fold_in(own_key, 6)
    for position, blocks in cuts:
        draws = jnp.exp(jax.random.uniform(jax.random.fold_in(own, position), (blocks,), jnp.float32, smallest / len(cuts), top_value / len(cuts)))
        level = level * jnp.repeat(draws, shape[position] // blocks).reshape([-1 if axis == position else 1 for axis in range(len(shape))])
    return level


def centred(own_key, shape, deviation, bound, split=(), kind=jnp.bfloat16):
    entries = deviation * jax.random.normal(own_key, shape, jnp.float32)
    if split:
        entries = entries * levels(own_key, shape, split, -0.22, 0.18)
    return jnp.clip(entries, -bound, bound).astype(kind)


def setup_inputs(seed: int = 0) -> dict:
    key_of = jax.random.split(jax.random.key(seed), 7)
    query = centred(key_of[0], (LEN, CH), 1.0, 6.0, ((0, 512),))
    keys = centred(key_of[1], (LEN, CH), 1.0, 6.0, ((0, 512),))
    values = centred(key_of[2], (LEN, CH), 1.0, 6.0, ((0, 512),))
    decay = jnp.clip(jnp.exp(math.log(0.03) - 8.970091 * jax.random.uniform(key_of[3], (GROUPS, ORDER), jnp.float32) ** levels(key_of[3], (GROUPS, ORDER), ((0, 16),), -0.2, 0.2)), 3.814697265625e-06, 0.03)
    residue = centred(key_of[4], (GROUPS, ORDER), 0.25, 2.5, ((0, 16),), jnp.float32)
    skip = jnp.clip(0.5 + 1.0 * jax.random.uniform(key_of[5], (CH,), jnp.float32) ** levels(key_of[5], (CH,), ((0, 16),), -0.2, 0.2), 0.5, 1.5)
    return {"query": query, "keys": keys, "values": values, "decay": decay, "residue": residue, "skip": skip}


def reference(query, keys, values, decay, residue, skip):
    product = (keys.astype(jnp.float32) * values.astype(jnp.float32)).astype(jnp.bfloat16)
    positions = jnp.arange(LEN, dtype=jnp.float32)
    amplitude = residue * jnp.sqrt(2.0 * decay)

    def one_filter(pieces):
        amp_row, rate_row = pieces
        return lax.optimization_barrier(jnp.sum(amp_row[:, None] * jnp.exp(-rate_row[:, None] * positions[None, :]), axis=0))
    filters = lax.map(one_filter, (amplitude, decay))
    spectra = jnp.fft.rfft(filters, n=2 * LEN, axis=-1)
    signal = product.astype(jnp.float32).T.reshape(GROUPS, GSZ, LEN)

    def one_group(pieces):
        rows_in, spectrum = pieces
        return jnp.fft.irfft(jnp.fft.rfft(rows_in, n=2 * LEN, axis=-1) * spectrum[None, :], n=2 * LEN, axis=-1)[:, :LEN]
    conv = lax.map(one_group, (signal, spectra)).reshape(CH, LEN)
    mixed = (conv + skip[:, None] * product.astype(jnp.float32).T).astype(jnp.bfloat16)
    return (query.astype(jnp.float32) * mixed.T.astype(jnp.float32)).astype(jnp.bfloat16)
```

```python
import functools

import jax
import jax.numpy as jnp
from jax import lax
from jax.experimental import pallas as pl
from jax.experimental.pallas import tpu as pltpu
from jax.sharding import PartitionSpec as P

F32 = jnp.float32
BF16 = jnp.bfloat16
VMEM = pl.BlockSpec(memory_space=pltpu.VMEM)
SMEM = pl.BlockSpec(memory_space=pltpu.SMEM)
NT = (((1,), (1,)), ((), ()))


def call(body, out_shape, in_specs, flops, nbytes, **kw):
    return pl.pallas_call(
        body,
        out_shape=out_shape,
        in_specs=in_specs,
        out_specs=jax.tree.map(lambda _: VMEM, out_shape),
        cost_estimate=pl.CostEstimate(flops=flops, bytes_accessed=nbytes, transcendentals=0),
        **kw,
    )


def split(table):
    high = table.astype(BF16)
    return high, (table - high.astype(F32)).astype(BF16)


def dot(a, b):
    return jnp.dot(a, b, preferred_element_type=F32)


def own_group(shape, group_rows, modes):
    row = lax.broadcasted_iota(jnp.int32, shape, len(shape) - 2)
    lane = lax.broadcasted_iota(jnp.int32, shape, len(shape) - 1)
    return (row // group_rows) == (lane // modes)


def gate_in_kernel(keys_ref, values_ref, out_ref):
    z = keys_ref[...].astype(F32) * values_ref[...].astype(F32)
    out_ref[...] = z.T.astype(BF16).reshape(out_ref.shape)


def table_kernel(dims, seq_ref, decay_ref, high_ref, low_ref, step_ref, grow_ref, seq_w_ref):
    blocks, rows, length, modes, group_rows = dims
    decay = decay_ref[...]
    lanes = decay.shape[1]
    back = (length - 1) - lax.broadcasted_iota(jnp.int32, (length, lanes), 0)
    high, low = split(jnp.exp(-decay * back.astype(F32)))
    high_ref[...] = high
    low_ref[...] = low
    step_ref[...] = jnp.exp(-decay * float(length))
    shape = (blocks, rows, lanes)
    block = lax.broadcasted_iota(jnp.int32, shape, 0)
    grow = jnp.exp(-decay[None] * (block * length).astype(F32))
    grow_ref[...] = jnp.where(own_group(shape, group_rows, modes), grow, 0.0)
    shape = seq_w_ref.shape
    gap = seq_ref[0] - 1 - lax.broadcasted_iota(jnp.int32, shape, 0)
    away = jnp.maximum(gap, 0) * (blocks * length)
    seq_w_ref[...] = jnp.where(gap >= 0, jnp.exp(-decay[None] * away.astype(F32)), 0.0)


def state_kernel(dims, z_ref, high_ref, low_ref, step_ref, state_ref, end_ref):
    blocks, rows, length, modes, group_rows = dims
    z = z_ref[...].reshape(blocks * rows, length)
    ends = dot(z, high_ref[...]) + dot(z, low_ref[...])
    lanes = ends.shape[1]
    mine = own_group((rows, lanes), group_rows, modes)
    step = step_ref[...]
    state = jnp.zeros((rows, lanes), F32)
    for b in range(blocks):
        state_ref[b] = state
        state = state * step + jnp.where(mine, ends[b * rows : (b + 1) * rows], 0.0)
    folded = state[:group_rows]
    for g in range(1, rows // group_rows):
        folded = folded + state[g * group_rows : (g + 1) * group_rows]
    end_ref[...] = jnp.broadcast_to(folded[None], end_ref.shape)


def local_kernel(dims, z_ref, state_ref, decay_ref, residue_ref, skip_ref, out_ref, table_ref):
    blocks, rows, length, modes, group_rows = dims
    decay = decay_ref[...]
    lanes = decay.shape[1]
    amplitude = residue_ref[...] * jnp.sqrt(2.0 * decay)
    position = lax.broadcasted_iota(jnp.int32, (length, lanes), 0).astype(F32)
    rise = jnp.exp(decay * position)
    fall = amplitude * jnp.exp(-decay * position)
    after = amplitude * jnp.exp(-decay * (position + 1.0))
    table_ref[...] = after
    z = z_ref[...].reshape(blocks * rows, length)
    row = lax.broadcasted_iota(jnp.int32, (length, length), 0)
    col = lax.broadcasted_iota(jnp.int32, (length, length), 1)
    lane = lax.broadcasted_iota(jnp.int32, (length, lanes), 1)
    groups = rows // group_rows
    parts = []
    for g in range(groups):
        taps = lax.dot_general(
            jnp.where(lane // modes == g, rise, 0.0), fall, NT,
            precision=lax.Precision.HIGHEST, preferred_element_type=F32,
        )
        high, low = split(jnp.where(row <= col, taps, 0.0))
        conv = (dot(z, high) + dot(z, low)).reshape(blocks, groups, group_rows, length)
        parts.append(conv[:, g])
    local = jnp.stack(parts, axis=1).reshape(blocks, rows, length)
    carried = lax.dot_general(
        state_ref[...].reshape(blocks * rows, lanes), after, NT,
        precision=lax.Precision.HIGHEST, preferred_element_type=F32,
    ).reshape(blocks, rows, length)
    out_ref[...] = local + carried + skip_ref[...][None] * z_ref[...].astype(F32)


def carry_kernel(dims, ends_ref, seq_w_ref, grow_ref, table_ref, local_ref, out_ref):
    blocks, rows, length, modes, group_rows = dims
    enter = jnp.sum(ends_ref[...] * seq_w_ref[...], axis=0)
    lanes = enter.shape[1]
    groups = rows // group_rows
    enter = jnp.concatenate([enter] * groups, axis=0)
    state = (grow_ref[...] * enter[None]).reshape(blocks * rows, lanes)
    carried = lax.dot_general(
        state, table_ref[...], NT,
        precision=lax.Precision.HIGHEST, preferred_element_type=F32,
    ).reshape(blocks, rows, length)
    out_ref[...] = (local_ref[...] + carried).astype(BF16)


def gate_out_kernel(query_ref, mixed_ref, out_ref):
    chan, length = out_ref.shape[1], out_ref.shape[0]
    mixed = mixed_ref[...].reshape(chan, length).astype(F32).T
    out_ref[...] = (query_ref[...].astype(F32) * mixed).astype(BF16)


def on_device(query, keys, values, decay, residue, skip):
    seq_count = lax.axis_size("seq")
    blocks = lax.axis_size("chan")
    length, chan = query.shape
    rows = skip.shape[0]
    filters, modes = decay.shape
    group_rows = rows // filters
    lanes = filters * modes
    dims = (blocks, rows, length, modes, group_rows)
    shape = jax.ShapeDtypeStruct
    size = length * chan

    decay_row = decay.reshape(1, lanes)
    residue_row = residue.reshape(1, lanes)
    skip_col = skip.reshape(rows, 1)
    seq_index = lax.axis_index("seq").astype(jnp.int32).reshape(1)

    gated = call(
        gate_in_kernel, shape((blocks, rows, length), BF16), [VMEM] * 2, size, 6 * size
    )(keys, values)
    z = lax.all_to_all(gated, "chan", 0, 0, tiled=True)
    high, low, step, grow, seq_w = call(
        functools.partial(table_kernel, dims),
        (
            shape((length, lanes), BF16),
            shape((length, lanes), BF16),
            shape((1, lanes), F32),
            shape((blocks, rows, lanes), F32),
            shape((seq_count, group_rows, lanes), F32),
        ),
        [SMEM, VMEM], 100 * size, 8 * size,
    )(seq_index, decay_row)
    state, ends = call(
        functools.partial(state_kernel, dims),
        (shape((blocks, rows, lanes), F32), shape((seq_count, group_rows, lanes), F32)),
        [VMEM] * 4, 4 * lanes * size, 4 * size,
    )(z, high, low, step)
    ends = lax.all_to_all(ends, "seq", 0, 0, tiled=True)
    local, table = call(
        functools.partial(local_kernel, dims),
        (shape((blocks, rows, length), F32), shape((length, lanes), F32)),
        [VMEM] * 5, 8 * length * size, 8 * size,
    )(z, state, decay_row, residue_row, skip_col)
    mixed = call(
        functools.partial(carry_kernel, dims),
        shape((blocks, rows, length), BF16),
        [VMEM] * 5, 12 * lanes * size, 8 * size,
    )(ends, seq_w, grow, table, local)
    mixed = lax.all_to_all(mixed, "chan", 0, 0, tiled=True)
    return call(
        gate_out_kernel, shape((length, chan), BF16), [VMEM] * 2, size, 6 * size
    )(query, mixed)


def solution(mesh):
    tokens = P(("seq", "chan"), None)
    return jax.shard_map(
        on_device,
        mesh=mesh,
        in_specs=(tokens, tokens, tokens, P("chan", None), P("chan", None), P("chan")),
        out_specs=tokens,
        check_vma=False,
    )
```

```python
import functools

import jax
import jax.numpy as jnp
from jax import lax
from jax.experimental import pallas as pl
from jax.experimental.pallas import tpu as pltpu
from jax.sharding import PartitionSpec as P

F32 = jnp.float32
BF16 = jnp.bfloat16
VMEM = pl.BlockSpec(memory_space=pltpu.VMEM)
SMEM = pl.BlockSpec(memory_space=pltpu.SMEM)
NT = (((1,), (1,)), ((), ()))


def call(body, out_shape, in_specs, flops, nbytes, **kw):
    return pl.pallas_call(
        body,
        out_shape=out_shape,
        in_specs=in_specs,
        out_specs=jax.tree.map(lambda _: VMEM, out_shape),
        cost_estimate=pl.CostEstimate(flops=flops, bytes_accessed=nbytes, transcendentals=0),
        compiler_params=pltpu.CompilerParams(vmem_limit_bytes=16 << 20),
        **kw,
    )


def split(table):
    high = table.astype(BF16)
    return high, (table - high.astype(F32)).astype(BF16)


def dot(a, b):
    return jnp.dot(a, b, preferred_element_type=F32)


def own_group(shape, group_rows, modes):
    row = lax.broadcasted_iota(jnp.int32, shape, len(shape) - 2)
    lane = lax.broadcasted_iota(jnp.int32, shape, len(shape) - 1)
    return (row // group_rows) == (lane // modes)


def gate_in_kernel(keys_ref, values_ref, out_ref):
    z = keys_ref[...].astype(F32) * values_ref[...].astype(F32)
    out_ref[...] = z.T.astype(BF16).reshape(out_ref.shape)


def table_kernel(dims, seq_ref, decay_ref, high_ref, low_ref, step_ref, grow_ref, seq_w_ref):
    blocks, rows, length, modes, group_rows = dims
    decay = decay_ref[...]
    lanes = decay.shape[1]
    back = (length - 1) - lax.broadcasted_iota(jnp.int32, (length, lanes), 0)
    high, low = split(jnp.exp(-decay * back.astype(F32)))
    high_ref[...] = high
    low_ref[...] = low
    step_ref[...] = jnp.exp(-decay * float(length))
    shape = (blocks, rows, lanes)
    block = lax.broadcasted_iota(jnp.int32, shape, 0)
    grow = jnp.exp(-decay[None] * (block * length).astype(F32))
    grow_ref[...] = jnp.where(own_group(shape, group_rows, modes), grow, 0.0)
    shape = seq_w_ref.shape
    gap = seq_ref[0] - 1 - lax.broadcasted_iota(jnp.int32, shape, 0)
    away = jnp.maximum(gap, 0) * (blocks * length)
    seq_w_ref[...] = jnp.where(gap >= 0, jnp.exp(-decay[None] * away.astype(F32)), 0.0)


def state_kernel(dims, z_ref, high_ref, low_ref, step_ref, state_ref, end_ref):
    blocks, rows, length, modes, group_rows = dims
    z = z_ref[...].reshape(blocks * rows, length)
    ends = dot(z, high_ref[...]) + dot(z, low_ref[...])
    lanes = ends.shape[1]
    mine = own_group((rows, lanes), group_rows, modes)
    step = step_ref[...]
    state = jnp.zeros((rows, lanes), F32)
    for b in range(blocks):
        state_ref[b] = state
        state = state * step + jnp.where(mine, ends[b * rows : (b + 1) * rows], 0.0)
    folded = state[:group_rows]
    for g in range(1, rows // group_rows):
        folded = folded + state[g * group_rows : (g + 1) * group_rows]
    spare = jnp.zeros((group_rows, end_ref.shape[2] - lanes), F32)
    end_ref[...] = jnp.broadcast_to(jnp.concatenate([folded, spare], axis=1)[None], end_ref.shape)


def local_kernel(dims, z_ref, state_ref, decay_ref, residue_ref, skip_ref, out_ref, table_ref):
    blocks, rows, length, modes, group_rows = dims
    decay = decay_ref[...]
    lanes = decay.shape[1]
    amplitude = residue_ref[...] * jnp.sqrt(2.0 * decay)
    position = lax.broadcasted_iota(jnp.int32, (length, lanes), 0).astype(F32)
    rise = jnp.exp(decay * position)
    fall = amplitude * jnp.exp(-decay * position)
    after = amplitude * jnp.exp(-decay * (position + 1.0))
    table_ref[...] = after
    z = z_ref[...].reshape(blocks * rows, length)
    row = lax.broadcasted_iota(jnp.int32, (length, length), 0)
    col = lax.broadcasted_iota(jnp.int32, (length, length), 1)
    lane = lax.broadcasted_iota(jnp.int32, (length, lanes), 1)
    groups = rows // group_rows
    parts = []
    for g in range(groups):
        taps = lax.dot_general(
            jnp.where(lane // modes == g, rise, 0.0), fall, NT,
            precision=lax.Precision.HIGHEST, preferred_element_type=F32,
        )
        high, low = split(jnp.where(row <= col, taps, 0.0))
        conv = (dot(z, high) + dot(z, low)).reshape(blocks, groups, group_rows, length)
        parts.append(conv[:, g])
    local = jnp.stack(parts, axis=1).reshape(blocks, rows, length)
    carried = lax.dot_general(
        state_ref[...].reshape(blocks * rows, lanes), after, NT,
        precision=lax.Precision.HIGHEST, preferred_element_type=F32,
    ).reshape(blocks, rows, length)
    out_ref[...] = local + carried + skip_ref[...][None] * z_ref[...].astype(F32)


def carry_kernel(dims, ends_ref, seq_w_ref, grow_ref, table_ref, local_ref, out_ref):
    blocks, rows, length, modes, group_rows = dims
    lanes = grow_ref.shape[2]
    enter = jnp.sum(ends_ref[:, :, :lanes] * seq_w_ref[...], axis=0)
    groups = rows // group_rows
    enter = jnp.concatenate([enter] * groups, axis=0)
    state = (grow_ref[...] * enter[None]).reshape(blocks * rows, lanes)
    carried = lax.dot_general(
        state, table_ref[...], NT,
        precision=lax.Precision.HIGHEST, preferred_element_type=F32,
    ).reshape(blocks, rows, length)
    out_ref[...] = (local_ref[...] + carried).astype(BF16)


def gate_out_kernel(query_ref, mixed_ref, out_ref):
    chan, length = out_ref.shape[1], out_ref.shape[0]
    mixed = mixed_ref[...].reshape(chan, length).astype(F32).T
    out_ref[...] = (query_ref[...].astype(F32) * mixed).astype(BF16)


def on_device(query, keys, values, decay, residue, skip):
    seq_count = lax.axis_size("seq")
    blocks = lax.axis_size("chan")
    length, chan = query.shape
    rows = skip.shape[0]
    filters, modes = decay.shape
    group_rows = rows // filters
    lanes = filters * modes
    dims = (blocks, rows, length, modes, group_rows)
    shape = jax.ShapeDtypeStruct
    size = length * chan

    decay_row = decay.reshape(1, lanes)
    residue_row = residue.reshape(1, lanes)
    skip_col = skip.reshape(rows, 1)
    seq_index = lax.axis_index("seq").astype(jnp.int32).reshape(1)

    gated = call(
        gate_in_kernel, shape((blocks, rows, length), BF16), [VMEM] * 2, size, 6 * size
    )(keys, values)
    z = lax.all_to_all(gated, "chan", 0, 0, tiled=True)
    high, low, step, grow, seq_w = call(
        functools.partial(table_kernel, dims),
        (
            shape((length, lanes), BF16),
            shape((length, lanes), BF16),
            shape((1, lanes), F32),
            shape((blocks, rows, lanes), F32),
            shape((seq_count, group_rows, lanes), F32),
        ),
        [SMEM, VMEM], 100 * size, 8 * size,
    )(seq_index, decay_row)
    state, ends = call(
        functools.partial(state_kernel, dims),
        (shape((blocks, rows, lanes), F32), shape((seq_count, group_rows, 128), F32)),
        [VMEM] * 4, 4 * lanes * size, 4 * size,
    )(z, high, low, step)
    ends = lax.all_to_all(ends, "seq", 0, 0, tiled=True)
    local, table = call(
        functools.partial(local_kernel, dims),
        (shape((blocks, rows, length), F32), shape((length, lanes), F32)),
        [VMEM] * 5, 8 * length * size, 8 * size,
    )(z, state, decay_row, residue_row, skip_col)
    mixed = call(
        functools.partial(carry_kernel, dims),
        shape((blocks, rows, length), BF16),
        [VMEM] * 5, 12 * lanes * size, 8 * size,
    )(ends, seq_w, grow, table, local)
    mixed = lax.all_to_all(mixed, "chan", 0, 0, tiled=True)
    return call(
        gate_out_kernel, shape((length, chan), BF16), [VMEM] * 2, size, 6 * size
    )(query, mixed)


def solution(mesh):
    tokens = P(("seq", "chan"), None)
    return jax.shard_map(
        on_device,
        mesh=mesh,
        in_specs=(tokens, tokens, tokens, P("chan", None), P("chan", None), P("chan")),
        out_specs=tokens,
        check_vma=False,
    )
```

```python
import functools

import jax
import jax.numpy as jnp
from jax import lax
from jax.experimental import pallas as pl
from jax.experimental.pallas import tpu as pltpu
from jax.sharding import PartitionSpec as P

F32 = jnp.float32
BF16 = jnp.bfloat16
VMEM = pl.BlockSpec(memory_space=pltpu.VMEM)
SMEM = pl.BlockSpec(memory_space=pltpu.SMEM)
HBM = pl.BlockSpec(memory_space=pltpu.HBM)
NT = (((1,), (1,)), ((), ()))


def call(body, out_shape, in_specs, flops, nbytes, vmem=16, **kw):
    return pl.pallas_call(
        body,
        out_shape=out_shape,
        in_specs=in_specs,
        out_specs=jax.tree.map(lambda _: VMEM, out_shape),
        cost_estimate=pl.CostEstimate(flops=flops, bytes_accessed=nbytes, transcendentals=0),
        compiler_params=pltpu.CompilerParams(vmem_limit_bytes=vmem << 20),
        **kw,
    )


def split(table):
    high = table.astype(BF16)
    return high, (table - high.astype(F32)).astype(BF16)


def dot(a, b):
    return jnp.dot(a, b, preferred_element_type=F32)


def dot_nt(a, b):
    return lax.dot_general(
        a, b, NT, precision=lax.Precision.HIGHEST, preferred_element_type=F32
    )


def own_lanes(shape, modes):
    row = lax.broadcasted_iota(jnp.int32, shape, len(shape) - 2)
    lane = lax.broadcasted_iota(jnp.int32, shape, len(shape) - 1)
    return row == lane // modes


def gate_in_kernel(keys_ref, values_ref, out_ref, keys_buf, values_buf, sems):
    half = keys_buf.shape[1]
    copies = []
    for h in range(2):
        part = pl.ds(h * half, half)
        copies.append(
            [
                pltpu.make_async_copy(keys_ref.at[part], keys_buf.at[h], sems.at[h, 0]),
                pltpu.make_async_copy(values_ref.at[part], values_buf.at[h], sems.at[h, 1]),
            ]
        )
        for copy in copies[h]:
            copy.start()
    blocks, rows, _ = out_ref.shape
    for h in range(2):
        for copy in copies[h]:
            copy.wait()
        z = keys_buf[h].astype(F32) * values_buf[h].astype(F32)
        out_ref[:, :, h * half : (h + 1) * half] = z.T.astype(BF16).reshape(blocks, rows, half)


def table_kernel(dims, seq_ref, decay_ref, high_ref, low_ref, step_ref, grow_ref, seq_w_ref):
    blocks, groups, size, length, modes = dims
    decay = decay_ref[...]
    lanes = decay.shape[1]
    back = (length - 1) - lax.broadcasted_iota(jnp.int32, (length, lanes), 0)
    for g in range(groups):
        high, low = split(jnp.exp(-decay[g : g + 1] * back.astype(F32)))
        high_ref[:, g * lanes : (g + 1) * lanes] = high
        low_ref[:, g * lanes : (g + 1) * lanes] = low
    step_ref[...] = jnp.exp(-decay * float(length))
    shape = (blocks, size, lanes)
    block = lax.broadcasted_iota(jnp.int32, shape, 0)
    for g in range(groups):
        grow = jnp.exp(-decay[g : g + 1][None] * (block * length).astype(F32))
        grow_ref[:, g] = jnp.where(own_lanes(shape, modes), grow, 0.0)
    shape = seq_w_ref.shape
    gap = seq_ref[0] - 1 - lax.broadcasted_iota(jnp.int32, shape, 0)
    away = jnp.maximum(gap, 0) * (blocks * length)
    seq_w_ref[...] = jnp.where(gap >= 0, jnp.exp(-decay[None] * away.astype(F32)), 0.0)


def state_kernel(dims, z_ref, high_ref, low_ref, step_ref, state_ref, end_ref):
    blocks, groups, size, length, modes = dims
    z = z_ref[...].reshape(blocks * groups * size, length)
    ends = dot(z, high_ref[...]) + dot(z, low_ref[...])
    lanes = step_ref.shape[1]
    ends = ends.reshape(blocks, groups, size, groups * lanes)
    mine = own_lanes((size, lanes), modes)
    packed = []
    for g in range(groups):
        step = step_ref[g : g + 1]
        state = jnp.zeros((size, lanes), F32)
        for b in range(blocks):
            state_ref[b, g] = state
            state = state * step + jnp.where(mine, ends[b, g, :, g * lanes : (g + 1) * lanes], 0.0)
        packed.append(jnp.sum(state, axis=0, keepdims=True))
    packed = jnp.concatenate(packed, axis=0)
    end_ref[...] = jnp.broadcast_to(packed[None], end_ref.shape)


def local_kernel(dims, z_ref, state_ref, decay_ref, residue_ref, skip_ref, out_ref, table_ref):
    blocks, groups, size, length, modes = dims
    lanes = decay_ref.shape[1]
    z = z_ref[...].reshape(blocks * groups * size, length)
    skipped = skip_ref[...][None] * z_ref[...].astype(F32)
    skipped = skipped.reshape(blocks, groups, size, length)
    row = lax.broadcasted_iota(jnp.int32, (length, length), 0)
    col = lax.broadcasted_iota(jnp.int32, (length, length), 1)
    position = lax.broadcasted_iota(jnp.int32, (length, lanes), 0).astype(F32)
    first = lax.broadcasted_iota(jnp.int32, (length, lanes), 1) < modes
    for g in range(groups):
        decay = decay_ref[g : g + 1]
        amplitude = residue_ref[g : g + 1] * jnp.sqrt(2.0 * decay)
        rise = jnp.where(first, jnp.exp(decay * position), 0.0)
        fall = amplitude * jnp.exp(-decay * position)
        after = amplitude * jnp.exp(-decay * (position + 1.0))
        table_ref[g] = after
        high, low = split(jnp.where(row <= col, dot_nt(rise, fall), 0.0))
        conv = (dot(z, high) + dot(z, low)).reshape(blocks, groups, size, length)[:, g]
        carried = dot_nt(state_ref[:, g].reshape(blocks * size, lanes), after)
        out_ref[:, g] = conv + carried.reshape(blocks, size, length) + skipped[:, g]


def carry_kernel(dims, ends_ref, seq_w_ref, grow_ref, table_ref, local_ref, out_ref):
    blocks, groups, size, length, modes = dims
    enter = jnp.sum(ends_ref[...] * seq_w_ref[...], axis=0)
    lanes = enter.shape[1]
    mixed = []
    for g in range(groups):
        state = (grow_ref[:, g] * enter[g : g + 1][None]).reshape(blocks * size, lanes)
        carried = dot_nt(state, table_ref[g]).reshape(blocks, size, length)
        mixed.append(local_ref[:, g] + carried)
    mixed = jnp.stack(mixed, axis=1).reshape(blocks, groups * size, length)
    out_ref[...] = mixed.astype(BF16)


def gate_out_kernel(query_ref, mixed_ref, out_ref):
    chan, length = out_ref.shape[1], out_ref.shape[0]
    mixed = mixed_ref[...].reshape(chan, length).astype(F32).T
    out_ref[...] = (query_ref[...].astype(F32) * mixed).astype(BF16)


def on_device(query, keys, values, decay, residue, skip):
    seq_count = lax.axis_size("seq")
    blocks = lax.axis_size("chan")
    length, chan = query.shape
    rows = skip.shape[0]
    groups, modes = decay.shape
    size = rows // groups
    lanes = size * modes
    dims = (blocks, groups, size, length, modes)
    shape = jax.ShapeDtypeStruct
    whole = length * chan

    decay_row = jnp.tile(decay, (1, size))
    residue_row = jnp.tile(residue, (1, size))
    skip_col = skip.reshape(rows, 1)
    seq_index = lax.axis_index("seq").astype(jnp.int32).reshape(1)

    gated = call(
        gate_in_kernel, shape((blocks, rows, length), BF16), [HBM] * 2, whole, 6 * whole, 60,
        scratch_shapes=[
            pltpu.VMEM((2, length // 2, chan), BF16),
            pltpu.VMEM((2, length // 2, chan), BF16),
            pltpu.SemaphoreType.DMA((2, 2)),
        ],
    )(keys, values)
    z = lax.all_to_all(gated, "chan", 0, 0, tiled=True)
    high, low, step, grow, seq_w = call(
        functools.partial(table_kernel, dims),
        (
            shape((length, groups * lanes), BF16),
            shape((length, groups * lanes), BF16),
            shape((groups, lanes), F32),
            shape((blocks, groups, size, lanes), F32),
            shape((seq_count, groups, lanes), F32),
        ),
        [SMEM, VMEM], 100 * whole, 8 * whole,
    )(seq_index, decay_row)
    state, ends = call(
        functools.partial(state_kernel, dims),
        (shape((blocks, groups, size, lanes), F32), shape((seq_count, groups, lanes), F32)),
        [VMEM] * 4, 4 * lanes * whole, 4 * whole,
    )(z, high, low, step)
    ends = lax.all_to_all(ends, "seq", 0, 0, tiled=True)
    local, table = call(
        functools.partial(local_kernel, dims),
        (shape((blocks, groups, size, length), F32), shape((groups, length, lanes), F32)),
        [VMEM] * 5, 8 * length * whole, 8 * whole,
    )(z, state, decay_row, residue_row, skip_col)
    mixed = call(
        functools.partial(carry_kernel, dims),
        shape((blocks, rows, length), BF16),
        [VMEM] * 5, 12 * lanes * whole, 8 * whole,
    )(ends, seq_w, grow, table, local)
    mixed = lax.all_to_all(mixed, "chan", 0, 0, tiled=True)
    return call(
        gate_out_kernel, shape((length, chan), BF16), [VMEM] * 2, whole, 6 * whole
    )(query, mixed)


def solution(mesh):
    tokens = P(("seq", "chan"), None)
    return jax.shard_map(
        on_device,
        mesh=mesh,
        in_specs=(tokens, tokens, tokens, P("chan", None), P("chan", None), P("chan")),
        out_specs=tokens,
        check_vma=False,
    )
```

```python
import functools

import jax
import jax.numpy as jnp
from jax import lax
from jax.experimental import pallas as pl
from jax.experimental.pallas import tpu as pltpu
from jax.sharding import Mesh
from jax.sharding import PartitionSpec as P

F32 = jnp.float32
BF16 = jnp.bfloat16
VMEM = pl.BlockSpec(memory_space=pltpu.VMEM)
SMEM = pl.BlockSpec(memory_space=pltpu.SMEM)
HBM = pl.BlockSpec(memory_space=pltpu.HBM)
NT = (((1,), (1,)), ((), ()))
HALVES = 2


def call(body, out_shape, in_specs, flops, nbytes, vmem=16, **kw):
    return pl.pallas_call(
        body,
        out_shape=out_shape,
        in_specs=in_specs,
        out_specs=jax.tree.map(lambda _: VMEM, out_shape),
        cost_estimate=pl.CostEstimate(flops=flops, bytes_accessed=nbytes, transcendentals=0),
        compiler_params=pltpu.CompilerParams(vmem_limit_bytes=vmem << 20),
        **kw,
    )


def split(table):
    high = table.astype(BF16)
    return high, (table - high.astype(F32)).astype(BF16)


def dot(a, b):
    return jnp.dot(a, b, preferred_element_type=F32)


def dot_nt(a, b):
    return lax.dot_general(
        a, b, NT, precision=lax.Precision.HIGHEST, preferred_element_type=F32
    )


def own_lanes(shape, modes):
    row = lax.broadcasted_iota(jnp.int32, shape, len(shape) - 2)
    lane = lax.broadcasted_iota(jnp.int32, shape, len(shape) - 1)
    return row == lane // modes


def unpack(message_ref, size):
    message = message_ref[...].astype(F32)
    return jnp.concatenate([message[:, :size], message[:, size:]], axis=2)


def pack(data):
    half = data.shape[2] // 2
    return jnp.concatenate([data[:, :, :half], data[:, :, half:]], axis=1).astype(BF16)


def swap(data, outer):
    return data.reshape(outer, -1, *data.shape[1:]).swapaxes(0, 1).reshape(data.shape)


def gate_in_kernel(size, keys_ref, values_ref, out_ref, keys_buf, values_buf, sems):
    half = keys_buf.shape[1]
    copies = []
    for h in range(2):
        part = pl.ds(h * half, half)
        copies.append(
            [
                pltpu.make_async_copy(keys_ref.at[part], keys_buf.at[h], sems.at[h, 0]),
                pltpu.make_async_copy(values_ref.at[part], values_buf.at[h], sems.at[h, 1]),
            ]
        )
        for copy in copies[h]:
            copy.start()
    filters = out_ref.shape[0]
    parts = []
    for h in range(2):
        for copy in copies[h]:
            copy.wait()
        z = keys_buf[h].astype(F32) * values_buf[h].astype(F32)
        parts.append(z.T.reshape(filters, size, half))
    z = swap(jnp.concatenate(parts, axis=1), filters // HALVES)
    out_ref[...] = z.astype(BF16)


def own_filter(place_ref, table):
    rows = table.shape[0] // HALVES
    return jnp.where(place_ref[0] == 0, table[:rows], table[rows:])


def table_kernel(dims, place_ref, decay_ref, high_ref, low_ref, step_ref, grow_ref, away_ref):
    blocks, size, length, modes = dims
    decay = own_filter(place_ref, decay_ref[...])
    lanes = decay.shape[1]
    back = (length - 1) - lax.broadcasted_iota(jnp.int32, (length, lanes), 0)
    high, low = split(jnp.exp(-decay * back.astype(F32)))
    high_ref[...] = high
    low_ref[...] = low
    step_ref[...] = jnp.exp(-decay * float(length))
    shape = (blocks, size, lanes)
    block = lax.broadcasted_iota(jnp.int32, shape, 0)
    grow = jnp.exp(-decay[None] * (block * length).astype(F32))
    grow_ref[...] = jnp.where(own_lanes(shape, modes), grow, 0.0)
    shape = away_ref.shape
    gap = place_ref[1] - 1 - lax.broadcasted_iota(jnp.int32, shape, 0)
    gap = gap + shape[0] * lax.broadcasted_iota(jnp.int32, shape, 1)
    away = jnp.maximum(gap, 0) * (blocks * length)
    away_ref[...] = jnp.where(gap >= 0, jnp.exp(-decay[None] * away.astype(F32)), 0.0)


def state_kernel(dims, z_ref, high_ref, low_ref, step_ref, state_ref, end_ref):
    blocks, size, length, modes = dims
    z = unpack(z_ref, size).reshape(HALVES * blocks * size, length).astype(BF16)
    ends = dot(z, high_ref[...]) + dot(z, low_ref[...])
    lanes = step_ref.shape[1]
    ends = ends.reshape(HALVES, blocks, size, lanes)
    mine = own_lanes((size, lanes), modes)
    step = step_ref[...]
    packed = []
    for h in range(HALVES):
        state = jnp.zeros((size, lanes), F32)
        for b in range(blocks):
            state_ref[h, b] = state
            state = state * step + jnp.where(mine, ends[h, b], 0.0)
        packed.append(jnp.sum(state, axis=0, keepdims=True))
    packed = jnp.concatenate(packed, axis=0)
    end_ref[...] = jnp.broadcast_to(packed[None], end_ref.shape)


def local_kernel(
    dims, place_ref, z_ref, state_ref, decay_ref, residue_ref, skip_ref, out_ref, table_ref
):
    blocks, size, length, modes = dims
    decay = own_filter(place_ref, decay_ref[...])
    lanes = decay.shape[1]
    z = unpack(z_ref, size)
    skipped = own_filter(place_ref, skip_ref[...])[None] * z
    z = z.reshape(HALVES * blocks * size, length).astype(BF16)
    row = lax.broadcasted_iota(jnp.int32, (length, length), 0)
    col = lax.broadcasted_iota(jnp.int32, (length, length), 1)
    position = lax.broadcasted_iota(jnp.int32, (length, lanes), 0).astype(F32)
    first = lax.broadcasted_iota(jnp.int32, (length, lanes), 1) < modes
    amplitude = own_filter(place_ref, residue_ref[...]) * jnp.sqrt(2.0 * decay)
    rise = jnp.where(first, jnp.exp(decay * position), 0.0)
    fall = amplitude * jnp.exp(-decay * position)
    after = amplitude * jnp.exp(-decay * (position + 1.0))
    table_ref[...] = after
    high, low = split(jnp.where(row <= col, dot_nt(rise, fall), 0.0))
    states = state_ref[...].reshape(HALVES * blocks * size, lanes)
    local = dot(z, high) + dot(z, low) + dot_nt(states, after)
    out_ref[...] = local.reshape(HALVES * blocks, size, length) + skipped


def carry_kernel(dims, ends_ref, away_ref, grow_ref, table_ref, local_ref, out_ref):
    blocks, size, length, modes = dims
    first, second = ends_ref[:, 0], ends_ref[:, 1]
    same, across = away_ref[:, 0], away_ref[:, 1]
    enter = [
        jnp.sum(first * same, axis=0, keepdims=True),
        jnp.sum(first * across + second * same, axis=0, keepdims=True),
    ]
    lanes = same.shape[1]
    state = jnp.concatenate([grow_ref[...] * e[None] for e in enter], axis=0)
    carried = dot_nt(state.reshape(HALVES * blocks * size, lanes), table_ref[...])
    out_ref[...] = pack(local_ref[...] + carried.reshape(HALVES * blocks, size, length))


def gate_out_kernel(size, query_ref, mixed_ref, out_ref):
    length, chan = out_ref.shape
    half = length // 2
    mixed = swap(mixed_ref[...].astype(F32), HALVES)
    for h in range(2):
        part = mixed[:, h * size : (h + 1) * size].reshape(chan, half).T
        rows = slice(h * half, (h + 1) * half)
        out_ref[rows] = (query_ref[rows].astype(F32) * part).astype(BF16)


def on_device(query, keys, values, decay, residue, skip):
    seq_count = lax.axis_size("yc")
    blocks = lax.axis_size("chan")
    length, chan = query.shape
    modes = decay.shape[1]
    size = skip.shape[0] // HALVES
    lanes = size * modes
    count = HALVES * blocks
    dims = (blocks, size, length, modes)
    shape = jax.ShapeDtypeStruct
    whole = length * chan

    decay_row = jnp.tile(decay, (1, size))
    residue_row = jnp.tile(residue, (1, size))
    skip_col = skip.reshape(HALVES * size, 1)
    place = jnp.stack([lax.axis_index("zh"), lax.axis_index("yc")]).astype(jnp.int32)
    message = shape((count, 2 * size, length // 2), BF16)

    gated = call(
        functools.partial(gate_in_kernel, size), message, [HBM] * 2, whole, 6 * whole, 60,
        scratch_shapes=[
            pltpu.VMEM((2, length // 2, chan), BF16),
            pltpu.VMEM((2, length // 2, chan), BF16),
            pltpu.SemaphoreType.DMA((2, 2)),
        ],
    )(keys, values)
    z = lax.all_to_all(gated, ("zh", "chan"), 0, 0, tiled=True)
    high, low, step, grow, away = call(
        functools.partial(table_kernel, dims),
        (
            shape((length, lanes), BF16),
            shape((length, lanes), BF16),
            shape((1, lanes), F32),
            shape((blocks, size, lanes), F32),
            shape((seq_count, HALVES, lanes), F32),
        ),
        [SMEM, VMEM], 100 * whole, 8 * whole,
    )(place, decay_row)
    state, ends = call(
        functools.partial(state_kernel, dims),
        (shape((HALVES, blocks, size, lanes), F32), shape((seq_count, HALVES, lanes), F32)),
        [VMEM] * 4, 4 * lanes * whole, 4 * whole,
    )(z, high, low, step)
    ends = lax.all_to_all(ends, "yc", 0, 0, tiled=True)
    local, table = call(
        functools.partial(local_kernel, dims),
        (shape((count, size, length), F32), shape((length, lanes), F32)),
        [SMEM] + [VMEM] * 5, 8 * length * whole, 8 * whole,
    )(place, z, state, decay_row, residue_row, skip_col)
    mixed = call(
        functools.partial(carry_kernel, dims), message,
        [VMEM] * 5, 12 * lanes * whole, 8 * whole,
    )(ends, away, grow, table, local)
    mixed = lax.all_to_all(mixed, ("zh", "chan"), 0, 0, tiled=True)
    return call(
        functools.partial(gate_out_kernel, size), shape((length, chan), BF16),
        [VMEM] * 2, whole, 6 * whole,
    )(query, mixed)


def solution(mesh):
    chan = mesh.shape["chan"]
    cut = Mesh(mesh.devices.reshape(HALVES, -1, chan), ("zh", "yc", "chan"))
    tokens = P(("zh", "yc", "chan"), None)
    return jax.shard_map(
        on_device,
        mesh=cut,
        in_specs=(tokens, tokens, tokens, P("chan", None), P("chan", None), P("chan")),
        out_specs=tokens,
        check_vma=False,
    )
```

```python
import functools

import jax
import jax.numpy as jnp
from jax import lax
from jax.experimental import pallas as pl
from jax.experimental.pallas import tpu as pltpu
from jax.sharding import Mesh
from jax.sharding import PartitionSpec as P

F32 = jnp.float32
BF16 = jnp.bfloat16
VMEM = pl.BlockSpec(memory_space=pltpu.VMEM)
SMEM = pl.BlockSpec(memory_space=pltpu.SMEM)
HBM = pl.BlockSpec(memory_space=pltpu.HBM)
NT = (((1,), (1,)), ((), ()))
HALVES = 2


def call(body, out_shape, in_specs, flops, nbytes, vmem=16, **kw):
    return pl.pallas_call(
        body,
        out_shape=out_shape,
        in_specs=in_specs,
        out_specs=jax.tree.map(lambda _: VMEM, out_shape),
        cost_estimate=pl.CostEstimate(flops=flops, bytes_accessed=nbytes, transcendentals=0),
        compiler_params=pltpu.CompilerParams(vmem_limit_bytes=vmem << 20),
        **kw,
    )


def split(table):
    high = table.astype(BF16)
    return high, (table - high.astype(F32)).astype(BF16)


def dot(a, b):
    return jnp.dot(a, b, preferred_element_type=F32)


def dot_nt(a, b):
    return lax.dot_general(
        a, b, NT, precision=lax.Precision.HIGHEST, preferred_element_type=F32
    )


def own_lanes(shape, modes):
    row = lax.broadcasted_iota(jnp.int32, shape, len(shape) - 2)
    lane = lax.broadcasted_iota(jnp.int32, shape, len(shape) - 1)
    return row == lane // modes


def gate_in_kernel(keys_ref, values_ref, out_ref, keys_buf, values_buf, sems):
    half = keys_buf.shape[1]
    copies = []
    for h in range(2):
        part = pl.ds(h * half, half)
        copies.append(
            [
                pltpu.make_async_copy(keys_ref.at[part], keys_buf.at[h], sems.at[h, 0]),
                pltpu.make_async_copy(values_ref.at[part], values_buf.at[h], sems.at[h, 1]),
            ]
        )
        for copy in copies[h]:
            copy.start()
    blocks, rows, _ = out_ref.shape
    for h in range(2):
        for copy in copies[h]:
            copy.wait()
        z = keys_buf[h].astype(F32) * values_buf[h].astype(F32)
        out_ref[:, :, h * half : (h + 1) * half] = z.T.astype(BF16).reshape(blocks, rows, half)


def table_kernel(
    dims, place_ref, decay_ref, high_ref, low_ref, step_ref, grow_ref, inside_ref, whole_ref, cross_ref
):
    blocks, groups, size, length, modes = dims
    decay = decay_ref[...]
    lanes = decay.shape[1]
    back = (length - 1) - lax.broadcasted_iota(jnp.int32, (length, lanes), 0)
    for g in range(groups):
        high, low = split(jnp.exp(-decay[g : g + 1] * back.astype(F32)))
        high_ref[:, g * lanes : (g + 1) * lanes] = high
        low_ref[:, g * lanes : (g + 1) * lanes] = low
    step_ref[...] = jnp.exp(-decay * float(length))
    shape = (blocks, size, lanes)
    block = lax.broadcasted_iota(jnp.int32, shape, 0)
    for g in range(groups):
        grow = jnp.exp(-decay[g : g + 1][None] * (block * length).astype(F32))
        grow_ref[:, g] = jnp.where(own_lanes(shape, modes), grow, 0.0)
    shape = inside_ref.shape
    span = blocks * length
    place = place_ref[0]
    index = lax.broadcasted_iota(jnp.int32, shape, 0)
    gap = place - 1 - index
    away = jnp.maximum(gap, 0) * span
    inside_ref[...] = jnp.where(gap >= 0, jnp.exp(-decay[None] * away.astype(F32)), 0.0)
    left = (shape[0] - 1 - index) * span
    whole_ref[...] = jnp.exp(-decay[None] * left.astype(F32))
    cross_ref[...] = jnp.exp(-decay * (place * span).astype(F32))


def state_kernel(dims, z_ref, high_ref, low_ref, step_ref, state_ref, end_ref):
    blocks, groups, size, length, modes = dims
    z = z_ref[...].reshape(blocks * groups * size, length)
    ends = dot(z, high_ref[...]) + dot(z, low_ref[...])
    lanes = step_ref.shape[1]
    ends = ends.reshape(blocks, groups, size, groups * lanes)
    mine = own_lanes((size, lanes), modes)
    packed = []
    for g in range(groups):
        step = step_ref[g : g + 1]
        state = jnp.zeros((size, lanes), F32)
        for b in range(blocks):
            state_ref[b, g] = state
            state = state * step + jnp.where(mine, ends[b, g, :, g * lanes : (g + 1) * lanes], 0.0)
        packed.append(jnp.sum(state, axis=0, keepdims=True))
    packed = jnp.concatenate(packed, axis=0)
    end_ref[...] = jnp.broadcast_to(packed[None], end_ref.shape)


def local_kernel(dims, z_ref, state_ref, decay_ref, residue_ref, skip_ref, out_ref, table_ref):
    blocks, groups, size, length, modes = dims
    lanes = decay_ref.shape[1]
    z = z_ref[...].reshape(blocks * groups * size, length)
    skipped = skip_ref[...][None] * z_ref[...].astype(F32)
    skipped = skipped.reshape(blocks, groups, size, length)
    row = lax.broadcasted_iota(jnp.int32, (length, length), 0)
    col = lax.broadcasted_iota(jnp.int32, (length, length), 1)
    position = lax.broadcasted_iota(jnp.int32, (length, lanes), 0).astype(F32)
    first = lax.broadcasted_iota(jnp.int32, (length, lanes), 1) < modes
    for g in range(groups):
        decay = decay_ref[g : g + 1]
        amplitude = residue_ref[g : g + 1] * jnp.sqrt(2.0 * decay)
        rise = jnp.where(first, jnp.exp(decay * position), 0.0)
        fall = amplitude * jnp.exp(-decay * position)
        after = amplitude * jnp.exp(-decay * (position + 1.0))
        table_ref[g] = after
        high, low = split(jnp.where(row <= col, dot_nt(rise, fall), 0.0))
        conv = (dot(z, high) + dot(z, low)).reshape(blocks, groups, size, length)[:, g]
        carried = dot_nt(state_ref[:, g].reshape(blocks * size, lanes), after)
        out_ref[:, g] = conv + carried.reshape(blocks, size, length) + skipped[:, g]


def join_kernel(ends_ref, inside_ref, whole_ref, enter_ref, total_ref):
    ends = ends_ref[...]
    enter_ref[...] = jnp.sum(ends * inside_ref[...], axis=0)
    total_ref[...] = jnp.sum(ends * whole_ref[...], axis=0)


def carry_kernel(
    dims, enter_ref, before_ref, cross_ref, grow_ref, table_ref, local_ref, out_ref
):
    blocks, groups, size, length, modes = dims
    enter = enter_ref[...] + before_ref[...] * cross_ref[...]
    lanes = enter.shape[1]
    mixed = []
    for g in range(groups):
        state = (grow_ref[:, g] * enter[g : g + 1][None]).reshape(blocks * size, lanes)
        carried = dot_nt(state, table_ref[g]).reshape(blocks, size, length)
        mixed.append(local_ref[:, g] + carried)
    mixed = jnp.stack(mixed, axis=1).reshape(blocks, groups * size, length)
    out_ref[...] = mixed.astype(BF16)


def gate_out_kernel(query_ref, mixed_ref, out_ref):
    chan, length = out_ref.shape[1], out_ref.shape[0]
    mixed = mixed_ref[...].reshape(chan, length).astype(F32).T
    out_ref[...] = (query_ref[...].astype(F32) * mixed).astype(BF16)


def on_device(query, keys, values, decay, residue, skip):
    seq_count = lax.axis_size("yc")
    blocks = lax.axis_size("chan")
    length, chan = query.shape
    rows = skip.shape[0]
    groups, modes = decay.shape
    size = rows // groups
    lanes = size * modes
    dims = (blocks, groups, size, length, modes)
    shape = jax.ShapeDtypeStruct
    whole = length * chan

    decay_row = jnp.tile(decay, (1, size))
    residue_row = jnp.tile(residue, (1, size))
    skip_col = skip.reshape(rows, 1)
    place = lax.axis_index("yc").astype(jnp.int32).reshape(1)

    gated = call(
        gate_in_kernel, shape((blocks, rows, length), BF16), [HBM] * 2, whole, 6 * whole, 60,
        scratch_shapes=[
            pltpu.VMEM((2, length // 2, chan), BF16),
            pltpu.VMEM((2, length // 2, chan), BF16),
            pltpu.SemaphoreType.DMA((2, 2)),
        ],
    )(keys, values)
    z = lax.all_to_all(gated, "chan", 0, 0, tiled=True)
    high, low, step, grow, inside, whole_w, cross = call(
        functools.partial(table_kernel, dims),
        (
            shape((length, groups * lanes), BF16),
            shape((length, groups * lanes), BF16),
            shape((groups, lanes), F32),
            shape((blocks, groups, size, lanes), F32),
            shape((seq_count, groups, lanes), F32),
            shape((seq_count, groups, lanes), F32),
            shape((groups, lanes), F32),
        ),
        [SMEM, VMEM], 100 * whole, 8 * whole,
    )(place, decay_row)
    state, ends = call(
        functools.partial(state_kernel, dims),
        (shape((blocks, groups, size, lanes), F32), shape((seq_count, groups, lanes), F32)),
        [VMEM] * 4, 4 * lanes * whole, 4 * whole,
    )(z, high, low, step)
    ends = lax.all_to_all(ends, "yc", 0, 0, tiled=True)
    local, table = call(
        functools.partial(local_kernel, dims),
        (shape((blocks, groups, size, length), F32), shape((groups, length, lanes), F32)),
        [VMEM] * 5, 8 * length * whole, 8 * whole,
    )(z, state, decay_row, residue_row, skip_col)
    enter, total = call(
        join_kernel, (shape((groups, lanes), F32), shape((groups, lanes), F32)),
        [VMEM] * 3, 4 * seq_count * groups * lanes, 12 * seq_count * groups * lanes,
    )(ends, inside, whole_w)
    before = lax.ppermute(total, "zh", [(0, 1)])
    mixed = call(
        functools.partial(carry_kernel, dims),
        shape((blocks, rows, length), BF16),
        [VMEM] * 6, 12 * lanes * whole, 8 * whole,
    )(enter, before, cross, grow, table, local)
    mixed = lax.all_to_all(mixed, "chan", 0, 0, tiled=True)
    return call(
        gate_out_kernel, shape((length, chan), BF16), [VMEM] * 2, whole, 6 * whole
    )(query, mixed)


def solution(mesh):
    chan = mesh.shape["chan"]
    cut = Mesh(mesh.devices.reshape(HALVES, -1, chan), ("zh", "yc", "chan"))
    tokens = P(("zh", "yc", "chan"), None)
    return jax.shard_map(
        on_device,
        mesh=cut,
        in_specs=(tokens, tokens, tokens, P("chan", None), P("chan", None), P("chan")),
        out_specs=tokens,
        check_vma=False,
    )
```

```python
import functools

import jax
import jax.numpy as jnp
from jax import lax
from jax.experimental import pallas as pl
from jax.experimental.pallas import tpu as pltpu
from jax.sharding import Mesh
from jax.sharding import PartitionSpec as P

F32 = jnp.float32
BF16 = jnp.bfloat16
VMEM = pl.BlockSpec(memory_space=pltpu.VMEM)
SMEM = pl.BlockSpec(memory_space=pltpu.SMEM)
HBM = pl.BlockSpec(memory_space=pltpu.HBM)
NT = (((1,), (1,)), ((), ()))
HALVES = 2


def call(body, out_shape, in_specs, flops, nbytes, vmem=16, **kw):
    return pl.pallas_call(
        body,
        out_shape=out_shape,
        in_specs=in_specs,
        out_specs=jax.tree.map(lambda _: VMEM, out_shape),
        cost_estimate=pl.CostEstimate(flops=flops, bytes_accessed=nbytes, transcendentals=0),
        compiler_params=pltpu.CompilerParams(vmem_limit_bytes=vmem << 20),
        **kw,
    )


def split(table):
    high = table.astype(BF16)
    return high, (table - high.astype(F32)).astype(BF16)


def dot(a, b):
    return jnp.dot(a, b, preferred_element_type=F32)


def dot_nt(a, b):
    return lax.dot_general(
        a, b, NT, precision=lax.Precision.HIGHEST, preferred_element_type=F32
    )


def own_lanes(shape, modes):
    row = lax.broadcasted_iota(jnp.int32, shape, len(shape) - 2)
    lane = lax.broadcasted_iota(jnp.int32, shape, len(shape) - 1)
    return row == lane // modes


def gate_in_kernel(keys_ref, values_ref, out_ref, keys_buf, values_buf, sems):
    half = keys_buf.shape[1]
    copies = []
    for h in range(2):
        part = pl.ds(h * half, half)
        copies.append(
            [
                pltpu.make_async_copy(keys_ref.at[part], keys_buf.at[h], sems.at[h, 0]),
                pltpu.make_async_copy(values_ref.at[part], values_buf.at[h], sems.at[h, 1]),
            ]
        )
        for copy in copies[h]:
            copy.start()
    blocks, rows, _ = out_ref.shape
    for h in range(2):
        for copy in copies[h]:
            copy.wait()
        z = keys_buf[h].astype(F32) * values_buf[h].astype(F32)
        out_ref[:, :, h * half : (h + 1) * half] = z.T.astype(BF16).reshape(blocks, rows, half)


def table_kernel(
    dims, place_ref, decay_ref, residue_ref,
    high_ref, low_ref, step_ref, grow_ref, inside_ref, whole_ref, cross_ref,
    conv_high_ref, conv_low_ref, after_ref,
):
    blocks, groups, size, length, modes = dims
    decay = decay_ref[...]
    lanes = decay.shape[1]
    row = lax.broadcasted_iota(jnp.int32, (length, length), 0)
    col = lax.broadcasted_iota(jnp.int32, (length, length), 1)
    position = lax.broadcasted_iota(jnp.int32, (length, lanes), 0).astype(F32)
    first = lax.broadcasted_iota(jnp.int32, (length, lanes), 1) < modes
    shape = (blocks, size, lanes)
    block = lax.broadcasted_iota(jnp.int32, shape, 0)
    for g in range(groups):
        rate = decay[g : g + 1]
        high, low = split(jnp.exp(-rate * ((length - 1) - position)))
        high_ref[g] = high
        low_ref[g] = low
        grow = jnp.exp(-rate[None] * (block * length).astype(F32))
        grow_ref[:, g] = jnp.where(own_lanes(shape, modes), grow, 0.0)
        amplitude = residue_ref[g : g + 1] * jnp.sqrt(2.0 * rate)
        rise = jnp.where(first, jnp.exp(rate * position), 0.0)
        fall = amplitude * jnp.exp(-rate * position)
        high, low = split(jnp.where(row <= col, dot_nt(rise, fall), 0.0))
        conv_high_ref[g] = high
        conv_low_ref[g] = low
        after_ref[g] = amplitude * jnp.exp(-rate * (position + 1.0))
    step_ref[...] = jnp.exp(-decay * float(length))
    shape = inside_ref.shape
    span = blocks * length
    place = place_ref[0]
    index = lax.broadcasted_iota(jnp.int32, shape, 0)
    gap = place - 1 - index
    away = jnp.maximum(gap, 0) * span
    inside_ref[...] = jnp.where(gap >= 0, jnp.exp(-decay[None] * away.astype(F32)), 0.0)
    left = (shape[0] - 1 - index) * span
    whole_ref[...] = jnp.exp(-decay[None] * left.astype(F32))
    cross_ref[...] = jnp.exp(-decay * (place * span).astype(F32))


def block_kernel(
    dims, z_ref, high_ref, low_ref, step_ref, conv_high_ref, conv_low_ref, after_ref, skip_ref,
    end_ref, out_ref, state_ref,
):
    blocks, groups, size, length, modes = dims
    lanes = step_ref.shape[1]
    z = z_ref[...].astype(F32)
    skipped = (skip_ref[...][None] * z).reshape(blocks, groups, size, length)
    z = z.reshape(blocks, groups, size, length)
    mine = own_lanes((size, lanes), modes)
    packed = []
    for g in range(groups):
        rows = z[:, g].reshape(blocks * size, length).astype(BF16)
        ends = (dot(rows, high_ref[g]) + dot(rows, low_ref[g])).reshape(blocks, size, lanes)
        step = step_ref[g : g + 1]
        state = jnp.zeros((size, lanes), F32)
        for b in range(blocks):
            state_ref[b] = state
            state = state * step + jnp.where(mine, ends[b], 0.0)
        packed.append(jnp.sum(state, axis=0, keepdims=True))
        conv = dot(rows, conv_high_ref[g]) + dot(rows, conv_low_ref[g])
        carried = dot_nt(state_ref[...].reshape(blocks * size, lanes), after_ref[g])
        out_ref[:, g] = (conv + carried).reshape(blocks, size, length) + skipped[:, g]
    packed = jnp.concatenate(packed, axis=0)
    end_ref[...] = jnp.broadcast_to(packed[None], end_ref.shape)


def total_kernel(ends_ref, whole_ref, total_ref):
    total_ref[...] = jnp.sum(ends_ref[...] * whole_ref[...], axis=0)


def carry_kernel(
    dims, ends_ref, inside_ref, before_ref, cross_ref, grow_ref, after_ref, local_ref, out_ref
):
    blocks, groups, size, length, modes = dims
    enter = jnp.sum(ends_ref[...] * inside_ref[...], axis=0)
    enter = enter + before_ref[...] * cross_ref[...]
    lanes = enter.shape[1]
    mixed = []
    for g in range(groups):
        state = (grow_ref[:, g] * enter[g : g + 1][None]).reshape(blocks * size, lanes)
        carried = dot_nt(state, after_ref[g]).reshape(blocks, size, length)
        mixed.append(local_ref[:, g] + carried)
    mixed = jnp.stack(mixed, axis=1).reshape(blocks, groups * size, length)
    out_ref[...] = mixed.astype(BF16)


def gate_out_kernel(query_ref, mixed_ref, out_ref):
    chan, length = out_ref.shape[1], out_ref.shape[0]
    mixed = mixed_ref[...].reshape(chan, length).astype(F32).T
    out_ref[...] = (query_ref[...].astype(F32) * mixed).astype(BF16)


def on_device(query, keys, values, decay, residue, skip):
    seq_count = lax.axis_size("yc")
    blocks = lax.axis_size("chan")
    length, chan = query.shape
    rows = skip.shape[0]
    groups, modes = decay.shape
    size = rows // groups
    lanes = size * modes
    dims = (blocks, groups, size, length, modes)
    shape = jax.ShapeDtypeStruct
    whole = length * chan

    decay_row = jnp.tile(decay, (1, size))
    residue_row = jnp.tile(residue, (1, size))
    skip_col = skip.reshape(rows, 1)
    place = lax.axis_index("yc").astype(jnp.int32).reshape(1)

    gated = call(
        gate_in_kernel, shape((blocks, rows, length), BF16), [HBM] * 2, whole, 6 * whole, 60,
        scratch_shapes=[
            pltpu.VMEM((2, length // 2, chan), BF16),
            pltpu.VMEM((2, length // 2, chan), BF16),
            pltpu.SemaphoreType.DMA((2, 2)),
        ],
    )(keys, values)
    z = lax.all_to_all(gated, "chan", 0, 0, tiled=True)
    table = shape((groups, length, lanes), BF16)
    conv_table = shape((groups, length, length), BF16)
    weights = shape((seq_count, groups, lanes), F32)
    vector = shape((groups, lanes), F32)
    high, low, step, grow, inside, total_w, cross, conv_high, conv_low, after = call(
        functools.partial(table_kernel, dims),
        (
            table, table, vector, shape((blocks, groups, size, lanes), F32),
            weights, weights, vector,
            conv_table, conv_table, shape((groups, length, lanes), F32),
        ),
        [SMEM, VMEM, VMEM], 100 * whole, 16 * whole,
    )(place, decay_row, residue_row)
    ends, local = call(
        functools.partial(block_kernel, dims),
        (weights, shape((blocks, groups, size, length), F32)),
        [VMEM] * 8, 8 * length * whole, 16 * whole,
        scratch_shapes=[pltpu.VMEM((blocks, size, lanes), F32)],
    )(z, high, low, step, conv_high, conv_low, after, skip_col)

    half = lax.axis_index("zh")
    exchange = lambda a: lax.all_to_all(a, "yc", 0, 0, tiled=True)
    keep = lambda a: a
    ends = lax.cond(half == 0, exchange, keep, ends)
    total = call(total_kernel, vector, [VMEM] * 2, whole, whole)(ends, total_w)
    before = lax.ppermute(total, "zh", [(0, 1)])
    ends = lax.cond(half == 1, exchange, keep, ends)
    mixed = call(
        functools.partial(carry_kernel, dims),
        shape((blocks, rows, length), BF16),
        [VMEM] * 7, 12 * lanes * whole, 8 * whole,
    )(ends, inside, before, cross, grow, after, local)
    mixed = lax.all_to_all(mixed, "chan", 0, 0, tiled=True)
    return call(
        gate_out_kernel, shape((length, chan), BF16), [VMEM] * 2, whole, 6 * whole
    )(query, mixed)


def solution(mesh):
    chan = mesh.shape["chan"]
    cut = Mesh(mesh.devices.reshape(HALVES, -1, chan), ("zh", "yc", "chan"))
    tokens = P(("zh", "yc", "chan"), None)
    return jax.shard_map(
        on_device,
        mesh=cut,
        in_specs=(tokens, tokens, tokens, P("chan", None), P("chan", None), P("chan")),
        out_specs=tokens,
        check_vma=False,
    )
```

```python
import functools

import jax
import jax.numpy as jnp
from jax import lax
from jax.experimental import pallas as pl
from jax.experimental.pallas import tpu as pltpu
from jax.sharding import Mesh
from jax.sharding import PartitionSpec as P

F32 = jnp.float32
BF16 = jnp.bfloat16
VMEM = pl.BlockSpec(memory_space=pltpu.VMEM)
SMEM = pl.BlockSpec(memory_space=pltpu.SMEM)
HBM = pl.BlockSpec(memory_space=pltpu.HBM)
NT = (((1,), (1,)), ((), ()))
HALVES = 2


def call(body, out_shape, in_specs, flops, nbytes, vmem=16, **kw):
    return pl.pallas_call(
        body,
        out_shape=out_shape,
        in_specs=in_specs,
        out_specs=jax.tree.map(lambda _: VMEM, out_shape),
        cost_estimate=pl.CostEstimate(flops=flops, bytes_accessed=nbytes, transcendentals=0),
        compiler_params=pltpu.CompilerParams(vmem_limit_bytes=vmem << 20),
        **kw,
    )


def split(table):
    high = table.astype(BF16)
    return high, (table - high.astype(F32)).astype(BF16)


def dot(a, b):
    return jnp.dot(a, b, preferred_element_type=F32)


def dot_nt(a, b):
    return lax.dot_general(
        a, b, NT, precision=lax.Precision.HIGHEST, preferred_element_type=F32
    )


def own_lanes(shape, modes):
    row = lax.broadcasted_iota(jnp.int32, shape, len(shape) - 2)
    lane = lax.broadcasted_iota(jnp.int32, shape, len(shape) - 1)
    return row == lane // modes


def gate_in_kernel(keys_ref, values_ref, out_ref, keys_buf, values_buf, sems):
    half = keys_buf.shape[1]
    copies = []
    for h in range(2):
        part = pl.ds(h * half, half)
        copies.append(
            [
                pltpu.make_async_copy(keys_ref.at[part], keys_buf.at[h], sems.at[h, 0]),
                pltpu.make_async_copy(values_ref.at[part], values_buf.at[h], sems.at[h, 1]),
            ]
        )
        for copy in copies[h]:
            copy.start()
    blocks, rows, _ = out_ref.shape
    for h in range(2):
        for copy in copies[h]:
            copy.wait()
        z = keys_buf[h].astype(F32) * values_buf[h].astype(F32)
        out_ref[:, :, h * half : (h + 1) * half] = z.T.astype(BF16).reshape(blocks, rows, half)


def table_kernel(
    dims, place_ref, decay_ref, residue_ref, query_ref,
    high_ref, low_ref, step_ref, grow_ref, inside_ref, whole_ref, cross_ref,
    conv_high_ref, conv_low_ref, after_ref, query_out_ref, sem,
):
    fetch = pltpu.make_async_copy(query_ref, query_out_ref, sem)
    fetch.start()
    blocks, groups, size, length, modes = dims
    decay = decay_ref[...]
    lanes = decay.shape[1]
    row = lax.broadcasted_iota(jnp.int32, (length, length), 0)
    col = lax.broadcasted_iota(jnp.int32, (length, length), 1)
    position = lax.broadcasted_iota(jnp.int32, (length, lanes), 0).astype(F32)
    first = lax.broadcasted_iota(jnp.int32, (length, lanes), 1) < modes
    shape = (blocks, size, lanes)
    block = lax.broadcasted_iota(jnp.int32, shape, 0)
    for g in range(groups):
        rate = decay[g : g + 1]
        high, low = split(jnp.exp(-rate * ((length - 1) - position)))
        high_ref[g] = high
        low_ref[g] = low
        grow = jnp.exp(-rate[None] * (block * length).astype(F32))
        grow_ref[:, g] = jnp.where(own_lanes(shape, modes), grow, 0.0)
        amplitude = residue_ref[g : g + 1] * jnp.sqrt(2.0 * rate)
        rise = jnp.where(first, jnp.exp(rate * position), 0.0)
        fall = amplitude * jnp.exp(-rate * position)
        high, low = split(jnp.where(row <= col, dot_nt(rise, fall), 0.0))
        conv_high_ref[g] = high
        conv_low_ref[g] = low
        after_ref[g] = amplitude * jnp.exp(-rate * (position + 1.0))
    step_ref[...] = jnp.exp(-decay * float(length))
    shape = inside_ref.shape
    span = blocks * length
    place = place_ref[0]
    index = lax.broadcasted_iota(jnp.int32, shape, 0)
    gap = place - 1 - index
    away = jnp.maximum(gap, 0) * span
    inside_ref[...] = jnp.where(gap >= 0, jnp.exp(-decay[None] * away.astype(F32)), 0.0)
    left = (shape[0] - 1 - index) * span
    whole_ref[...] = jnp.exp(-decay[None] * left.astype(F32))
    cross_ref[...] = jnp.exp(-decay * (place * span).astype(F32))
    fetch.wait()


def block_kernel(
    dims, z_ref, high_ref, low_ref, step_ref, conv_high_ref, conv_low_ref, after_ref, skip_ref,
    end_ref, out_ref, state_ref,
):
    blocks, groups, size, length, modes = dims
    lanes = step_ref.shape[1]
    z = z_ref[...].astype(F32)
    skipped = (skip_ref[...][None] * z).reshape(blocks, groups, size, length)
    z = z.reshape(blocks, groups, size, length)
    mine = own_lanes((size, lanes), modes)
    packed = []
    for g in range(groups):
        rows = z[:, g].reshape(blocks * size, length).astype(BF16)
        ends = (dot(rows, high_ref[g]) + dot(rows, low_ref[g])).reshape(blocks, size, lanes)
        step = step_ref[g : g + 1]
        state = jnp.zeros((size, lanes), F32)
        for b in range(blocks):
            state_ref[b] = state
            state = state * step + jnp.where(mine, ends[b], 0.0)
        packed.append(jnp.sum(state, axis=0, keepdims=True))
        conv = dot(rows, conv_high_ref[g]) + dot(rows, conv_low_ref[g])
        carried = dot_nt(state_ref[...].reshape(blocks * size, lanes), after_ref[g])
        out_ref[:, g] = (conv + carried).reshape(blocks, size, length) + skipped[:, g]
    packed = jnp.concatenate(packed, axis=0)
    end_ref[...] = jnp.broadcast_to(packed[None], end_ref.shape)


def total_kernel(ends_ref, whole_ref, total_ref):
    total_ref[...] = jnp.sum(ends_ref[...] * whole_ref[...], axis=0)


def add_carried(dims, enter, grow_ref, after_ref, local_ref, out_ref):
    blocks, groups, size, length, modes = dims
    lanes = enter.shape[1]
    mixed = []
    for g in range(groups):
        state = (grow_ref[:, g] * enter[g : g + 1][None]).reshape(blocks * size, lanes)
        carried = dot_nt(state, after_ref[g]).reshape(blocks, size, length)
        mixed.append(local_ref[:, g] + carried)
    mixed = jnp.stack(mixed, axis=1).reshape(blocks, groups * size, length)
    out_ref[...] = mixed.astype(BF16)


def carry_first_kernel(dims, ends_ref, inside_ref, *refs):
    add_carried(dims, jnp.sum(ends_ref[...] * inside_ref[...], axis=0), *refs)


def carry_second_kernel(dims, ends_ref, inside_ref, before_ref, cross_ref, *refs):
    enter = jnp.sum(ends_ref[...] * inside_ref[...], axis=0)
    add_carried(dims, enter + before_ref[...] * cross_ref[...], *refs)


def gate_out_kernel(query_ref, mixed_ref, out_ref):
    chan, length = out_ref.shape[1], out_ref.shape[0]
    mixed = mixed_ref[...].reshape(chan, length).astype(F32).T
    out_ref[...] = (query_ref[...].astype(F32) * mixed).astype(BF16)


def on_device(query, keys, values, decay, residue, skip):
    seq_count = lax.axis_size("yc")
    blocks = lax.axis_size("chan")
    length, chan = query.shape
    rows = skip.shape[0]
    groups, modes = decay.shape
    size = rows // groups
    lanes = size * modes
    dims = (blocks, groups, size, length, modes)
    shape = jax.ShapeDtypeStruct
    whole = length * chan

    decay_row = jnp.tile(decay, (1, size))
    residue_row = jnp.tile(residue, (1, size))
    skip_col = skip.reshape(rows, 1)
    place = lax.axis_index("yc").astype(jnp.int32).reshape(1)

    gated = call(
        gate_in_kernel, shape((blocks, rows, length), BF16), [HBM] * 2, whole, 6 * whole, 60,
        scratch_shapes=[
            pltpu.VMEM((2, length // 2, chan), BF16),
            pltpu.VMEM((2, length // 2, chan), BF16),
            pltpu.SemaphoreType.DMA((2, 2)),
        ],
    )(keys, values)
    z = lax.all_to_all(gated, "chan", 0, 0, tiled=True)
    table = shape((groups, length, lanes), BF16)
    conv_table = shape((groups, length, length), BF16)
    weights = shape((seq_count, groups, lanes), F32)
    vector = shape((groups, lanes), F32)
    high, low, step, grow, inside, total_w, cross, conv_high, conv_low, after, query_in = call(
        functools.partial(table_kernel, dims),
        (
            table, table, vector, shape((blocks, groups, size, lanes), F32),
            weights, weights, vector,
            conv_table, conv_table, shape((groups, length, lanes), F32),
            shape((length, chan), BF16),
        ),
        [SMEM, VMEM, VMEM, HBM], 100 * whole, 16 * whole,
        scratch_shapes=[pltpu.SemaphoreType.DMA],
    )(place, decay_row, residue_row, query)
    ends, local = call(
        functools.partial(block_kernel, dims),
        (weights, shape((blocks, groups, size, length), F32)),
        [VMEM] * 8, 8 * length * whole, 16 * whole,
        scratch_shapes=[pltpu.VMEM((blocks, size, lanes), F32)],
    )(z, high, low, step, conv_high, conv_low, after, skip_col)

    half = lax.axis_index("zh")
    exchange = lambda a: lax.all_to_all(a, "yc", 0, 0, tiled=True)
    ends = lax.cond(half == 0, exchange, lambda a: a, ends)
    total = call(total_kernel, vector, [VMEM] * 2, whole, whole)(ends, total_w)
    before = lax.ppermute(total, "zh", [(0, 1)])

    def finish(kernel, args):
        mixed = call(
            functools.partial(kernel, dims), shape((blocks, rows, length), BF16),
            [VMEM] * (len(args) + 3), 12 * lanes * whole, 8 * whole,
        )(*args, grow, after, local)
        return lax.all_to_all(mixed, "chan", 0, 0, tiled=True)

    def first_half(ends, mixed):
        return ends, finish(carry_first_kernel, (ends, inside))

    def second_half(ends, mixed):
        return exchange(ends), mixed

    ends, mixed = lax.cond(half == 0, first_half, second_half, ends, z)
    mixed = lax.cond(
        half == 1,
        lambda mixed, before: finish(carry_second_kernel, (ends, inside, before, cross)),
        lambda mixed, before: mixed,
        mixed, before,
    )
    return call(
        gate_out_kernel, shape((length, chan), BF16), [VMEM] * 2, whole, 6 * whole
    )(query_in, mixed)


def solution(mesh):
    chan = mesh.shape["chan"]
    cut = Mesh(mesh.devices.reshape(HALVES, -1, chan), ("zh", "yc", "chan"))
    tokens = P(("zh", "yc", "chan"), None)
    return jax.shard_map(
        on_device,
        mesh=cut,
        in_specs=(tokens, tokens, tokens, P("chan", None), P("chan", None), P("chan")),
        out_specs=tokens,
        check_vma=False,
    )
```

```python
import functools

import jax
import jax.numpy as jnp
from jax import lax
from jax.experimental import pallas as pl
from jax.experimental.pallas import tpu as pltpu
from jax.sharding import Mesh
from jax.sharding import PartitionSpec as P

F32 = jnp.float32
BF16 = jnp.bfloat16
VMEM = pl.BlockSpec(memory_space=pltpu.VMEM)
SMEM = pl.BlockSpec(memory_space=pltpu.SMEM)
HBM = pl.BlockSpec(memory_space=pltpu.HBM)
NT = (((1,), (1,)), ((), ()))
HALVES = 2

TOKENS_IN = [10, 11, 12, 0, 4, 3, 13, 2, 1, 7, 9, 15, 8, 14, 5, 6]
STATES = ([11, 8, 0, 4, 5, 15, 6, 7, 3, 12, 9, 1, 13, 2, 10, 14], [9, 8, 7, 13, 4, 0, 14, 12, 1, 3, 10, 11, 5, 6, 15, 2])
TOKENS_OUT = ([10, 13, 6, 0, 9, 8, 3, 12, 5, 11, 2, 1, 4, 15, 7, 14], [9, 3, 7, 14, 10, 13, 8, 1, 6, 15, 2, 5, 4, 11, 0, 12])


def call(body, out_shape, in_specs, flops, nbytes, vmem=16, **kw):
    return pl.pallas_call(
        body,
        out_shape=out_shape,
        in_specs=in_specs,
        out_specs=jax.tree.map(lambda _: VMEM, out_shape),
        cost_estimate=pl.CostEstimate(flops=flops, bytes_accessed=nbytes, transcendentals=0),
        compiler_params=pltpu.CompilerParams(vmem_limit_bytes=vmem << 20),
        **kw,
    )


def split(table):
    high = table.astype(BF16)
    return high, (table - high.astype(F32)).astype(BF16)


def dot(a, b):
    return jnp.dot(a, b, preferred_element_type=F32)


def dot_nt(a, b):
    return lax.dot_general(
        a, b, NT, precision=lax.Precision.HIGHEST, preferred_element_type=F32
    )


def own_lanes(shape, modes):
    row = lax.broadcasted_iota(jnp.int32, shape, len(shape) - 2)
    lane = lax.broadcasted_iota(jnp.int32, shape, len(shape) - 1)
    return row == lane // modes


def take(data, order):
    return jnp.stack([data[i] for i in order], axis=0)


def inverse(order):
    return [order.index(i) for i in range(len(order))]


def gate_in_kernel(order, keys_ref, values_ref, out_ref, keys_buf, values_buf, sems):
    half = keys_buf.shape[1]
    copies = []
    for h in range(2):
        part = pl.ds(h * half, half)
        copies.append(
            [
                pltpu.make_async_copy(keys_ref.at[part], keys_buf.at[h], sems.at[h, 0]),
                pltpu.make_async_copy(values_ref.at[part], values_buf.at[h], sems.at[h, 1]),
            ]
        )
        for copy in copies[h]:
            copy.start()
    blocks, rows, _ = out_ref.shape
    for h in range(2):
        for copy in copies[h]:
            copy.wait()
        z = keys_buf[h].astype(F32) * values_buf[h].astype(F32)
        z = take(z.T.reshape(blocks, rows, half), order)
        out_ref[:, :, h * half : (h + 1) * half] = z.astype(BF16)


def table_kernel(
    dims, orders, place_ref, decay_ref, residue_ref, query_ref,
    high_ref, low_ref, step_ref, grow_ref, inside_ref, whole_ref, cross_ref,
    conv_high_ref, conv_low_ref, after_ref, query_out_ref, sem,
):
    fetch = pltpu.make_async_copy(query_ref, query_out_ref, sem)
    fetch.start()
    blocks, groups, size, length, modes = dims
    decay = decay_ref[...]
    lanes = decay.shape[1]
    row = lax.broadcasted_iota(jnp.int32, (length, length), 0)
    col = lax.broadcasted_iota(jnp.int32, (length, length), 1)
    position = lax.broadcasted_iota(jnp.int32, (length, lanes), 0).astype(F32)
    first = lax.broadcasted_iota(jnp.int32, (length, lanes), 1) < modes
    shape = (blocks, size, lanes)
    block = lax.broadcasted_iota(jnp.int32, shape, 0)
    for g in range(groups):
        rate = decay[g : g + 1]
        high, low = split(jnp.exp(-rate * ((length - 1) - position)))
        high_ref[g] = high
        low_ref[g] = low
        grow = jnp.exp(-rate[None] * (block * length).astype(F32))
        grow_ref[:, g] = jnp.where(own_lanes(shape, modes), grow, 0.0)
        amplitude = residue_ref[g : g + 1] * jnp.sqrt(2.0 * rate)
        rise = jnp.where(first, jnp.exp(rate * position), 0.0)
        fall = amplitude * jnp.exp(-rate * position)
        high, low = split(jnp.where(row <= col, dot_nt(rise, fall), 0.0))
        conv_high_ref[g] = high
        conv_low_ref[g] = low
        after_ref[g] = amplitude * jnp.exp(-rate * (position + 1.0))
    step_ref[...] = jnp.exp(-decay * float(length))
    shape = inside_ref.shape
    span = blocks * length
    place = place_ref[0]
    message = lax.broadcasted_iota(jnp.int32, shape, 0)
    index = jnp.zeros(shape, jnp.int32)
    for b, members in enumerate(zip(*orders)):
        index = jnp.where(message == b, jnp.where(place_ref[1] == 0, *members), index)
    gap = place - 1 - index
    away = jnp.maximum(gap, 0) * span
    inside_ref[...] = jnp.where(gap >= 0, jnp.exp(-decay[None] * away.astype(F32)), 0.0)
    left = (shape[0] - 1 - index) * span
    whole_ref[...] = jnp.exp(-decay[None] * left.astype(F32))
    cross_ref[...] = jnp.exp(-decay * (place * span).astype(F32))
    fetch.wait()


def block_kernel(
    dims, order, z_ref, high_ref, low_ref, step_ref, conv_high_ref, conv_low_ref, after_ref, skip_ref,
    end_ref, out_ref, state_ref,
):
    blocks, groups, size, length, modes = dims
    lanes = step_ref.shape[1]
    z = take(z_ref[...].astype(F32), inverse(order))
    skipped = (skip_ref[...][None] * z).reshape(blocks, groups, size, length)
    z = z.reshape(blocks, groups, size, length)
    mine = own_lanes((size, lanes), modes)
    packed = []
    for g in range(groups):
        rows = z[:, g].reshape(blocks * size, length).astype(BF16)
        ends = (dot(rows, high_ref[g]) + dot(rows, low_ref[g])).reshape(blocks, size, lanes)
        step = step_ref[g : g + 1]
        state = jnp.zeros((size, lanes), F32)
        for b in range(blocks):
            state_ref[b] = state
            state = state * step + jnp.where(mine, ends[b], 0.0)
        packed.append(jnp.sum(state, axis=0, keepdims=True))
        conv = dot(rows, conv_high_ref[g]) + dot(rows, conv_low_ref[g])
        carried = dot_nt(state_ref[...].reshape(blocks * size, lanes), after_ref[g])
        out_ref[:, g] = (conv + carried).reshape(blocks, size, length) + skipped[:, g]
    packed = jnp.concatenate(packed, axis=0)
    end_ref[...] = jnp.broadcast_to(packed[None], end_ref.shape)


def total_kernel(ends_ref, whole_ref, total_ref):
    total_ref[...] = jnp.sum(ends_ref[...] * whole_ref[...], axis=0)


def add_carried(dims, order, enter, grow_ref, after_ref, local_ref, out_ref):
    blocks, groups, size, length, modes = dims
    lanes = enter.shape[1]
    mixed = []
    for g in range(groups):
        state = (grow_ref[:, g] * enter[g : g + 1][None]).reshape(blocks * size, lanes)
        carried = dot_nt(state, after_ref[g]).reshape(blocks, size, length)
        mixed.append(local_ref[:, g] + carried)
    mixed = jnp.stack(mixed, axis=1).reshape(blocks, groups * size, length)
    out_ref[...] = take(mixed, order).astype(BF16)


def carry_first_kernel(dims, order, ends_ref, inside_ref, *refs):
    add_carried(dims, order, jnp.sum(ends_ref[...] * inside_ref[...], axis=0), *refs)


def carry_second_kernel(dims, order, ends_ref, inside_ref, before_ref, cross_ref, *refs):
    enter = jnp.sum(ends_ref[...] * inside_ref[...], axis=0)
    add_carried(dims, order, enter + before_ref[...] * cross_ref[...], *refs)


def gate_out_kernel(orders, place_ref, query_ref, mixed_ref, out_ref):
    chan, length = out_ref.shape[1], out_ref.shape[0]

    def gate(order):
        mixed = take(mixed_ref[...].astype(F32), inverse(order)).reshape(chan, length).T
        out_ref[...] = (query_ref[...].astype(F32) * mixed).astype(BF16)

    for half, order in enumerate(orders):
        pl.when(place_ref[1] == half)(functools.partial(gate, order))


def on_device(query, keys, values, decay, residue, skip):
    seq_count = lax.axis_size("yc")
    blocks = lax.axis_size("chan")
    length, chan = query.shape
    rows = skip.shape[0]
    groups, modes = decay.shape
    size = rows // groups
    lanes = size * modes
    dims = (blocks, groups, size, length, modes)
    shape = jax.ShapeDtypeStruct
    whole = length * chan

    decay_row = jnp.tile(decay, (1, size))
    residue_row = jnp.tile(residue, (1, size))
    skip_col = skip.reshape(rows, 1)
    place = jnp.stack([lax.axis_index("yc"), lax.axis_index("zh")]).astype(jnp.int32)

    def exchange(axis, order):
        return lambda a: lax.all_to_all(
            a, axis, 0, 0, tiled=True, axis_index_groups=[list(order)]
        )

    gated = call(
        functools.partial(gate_in_kernel, TOKENS_IN), shape((blocks, rows, length), BF16),
        [HBM] * 2, whole, 6 * whole, 60,
        scratch_shapes=[
            pltpu.VMEM((2, length // 2, chan), BF16),
            pltpu.VMEM((2, length // 2, chan), BF16),
            pltpu.SemaphoreType.DMA((2, 2)),
        ],
    )(keys, values)
    z = exchange("chan", TOKENS_IN)(gated)
    table = shape((groups, length, lanes), BF16)
    conv_table = shape((groups, length, length), BF16)
    weights = shape((seq_count, groups, lanes), F32)
    vector = shape((groups, lanes), F32)
    high, low, step, grow, inside, total_w, cross, conv_high, conv_low, after, query_in = call(
        functools.partial(table_kernel, dims, STATES),
        (
            table, table, vector, shape((blocks, groups, size, lanes), F32),
            weights, weights, vector,
            conv_table, conv_table, shape((groups, length, lanes), F32),
            shape((length, chan), BF16),
        ),
        [SMEM, VMEM, VMEM, HBM], 100 * whole, 16 * whole,
        scratch_shapes=[pltpu.SemaphoreType.DMA],
    )(place, decay_row, residue_row, query)
    ends, local = call(
        functools.partial(block_kernel, dims, TOKENS_IN),
        (weights, shape((blocks, groups, size, length), F32)),
        [VMEM] * 8, 8 * length * whole, 16 * whole,
        scratch_shapes=[pltpu.VMEM((blocks, size, lanes), F32)],
    )(z, high, low, step, conv_high, conv_low, after, skip_col)

    half = lax.axis_index("zh")
    ends = lax.cond(half == 0, exchange("yc", STATES[0]), lambda a: a, ends)
    total = call(total_kernel, vector, [VMEM] * 2, whole, whole)(ends, total_w)
    before = lax.ppermute(total, "zh", [(0, 1)])

    def finish(kernel, order, args):
        mixed = call(
            functools.partial(kernel, dims, order), shape((blocks, rows, length), BF16),
            [VMEM] * (len(args) + 3), 12 * lanes * whole, 8 * whole,
        )(*args, grow, after, local)
        return exchange("chan", order)(mixed)

    def first_half(ends, mixed):
        return ends, finish(carry_first_kernel, TOKENS_OUT[0], (ends, inside))

    def second_half(ends, mixed):
        return exchange("yc", STATES[1])(ends), mixed

    def second_finish(mixed, before):
        return finish(carry_second_kernel, TOKENS_OUT[1], (ends, inside, before, cross))

    ends, mixed = lax.cond(half == 0, first_half, second_half, ends, z)
    mixed = lax.cond(half == 1, second_finish, lambda mixed, before: mixed, mixed, before)
    return call(
        functools.partial(gate_out_kernel, TOKENS_OUT), shape((length, chan), BF16),
        [SMEM] + [VMEM] * 2, whole, 6 * whole,
    )(place, query_in, mixed)


def solution(mesh):
    chan = mesh.shape["chan"]
    cut = Mesh(mesh.devices.reshape(HALVES, -1, chan), ("zh", "yc", "chan"))
    tokens = P(("zh", "yc", "chan"), None)
    return jax.shard_map(
        on_device,
        mesh=cut,
        in_specs=(tokens, tokens, tokens, P("chan", None), P("chan", None), P("chan")),
        out_specs=tokens,
        check_vma=False,
    )
```

```python
import functools

import jax
import jax.numpy as jnp
from jax import lax
from jax.experimental import pallas as pl
from jax.experimental.pallas import tpu as pltpu
from jax.sharding import Mesh
from jax.sharding import PartitionSpec as P

F32 = jnp.float32
BF16 = jnp.bfloat16
VMEM = pl.BlockSpec(memory_space=pltpu.VMEM)
SMEM = pl.BlockSpec(memory_space=pltpu.SMEM)
HBM = pl.BlockSpec(memory_space=pltpu.HBM)
NT = (((1,), (1,)), ((), ()))
HALVES = 2

TOKENS_IN = [10, 11, 12, 0, 4, 3, 13, 2, 1, 7, 9, 15, 8, 14, 5, 6]
STATES = [9, 8, 7, 13, 4, 0, 14, 12, 1, 3, 10, 11, 5, 6, 15, 2]
TOKENS_OUT = [10, 11, 12, 0, 4, 3, 13, 2, 1, 7, 9, 15, 8, 14, 5, 6]


def call(body, out_shape, in_specs, flops, nbytes, vmem=16, **kw):
    return pl.pallas_call(
        body,
        out_shape=out_shape,
        in_specs=in_specs,
        out_specs=jax.tree.map(lambda _: VMEM, out_shape),
        cost_estimate=pl.CostEstimate(flops=flops, bytes_accessed=nbytes, transcendentals=0),
        compiler_params=pltpu.CompilerParams(vmem_limit_bytes=vmem << 20),
        **kw,
    )


def split(table):
    high = table.astype(BF16)
    return high, (table - high.astype(F32)).astype(BF16)


def dot(a, b):
    return jnp.dot(a, b, preferred_element_type=F32)


def dot_nt(a, b):
    return lax.dot_general(
        a, b, NT, precision=lax.Precision.HIGHEST, preferred_element_type=F32
    )


def own_lanes(shape, modes):
    row = lax.broadcasted_iota(jnp.int32, shape, len(shape) - 2)
    lane = lax.broadcasted_iota(jnp.int32, shape, len(shape) - 1)
    return row == lane // modes


def take(data, order):
    return jnp.stack([data[i] for i in order], axis=0)


def inverse(order):
    return [order.index(i) for i in range(len(order))]


def gate_in_kernel(order, keys_ref, values_ref, out_ref, keys_buf, values_buf, sems):
    half = keys_buf.shape[1]
    copies = []
    for h in range(2):
        part = pl.ds(h * half, half)
        copies.append(
            [
                pltpu.make_async_copy(keys_ref.at[part], keys_buf.at[h], sems.at[h, 0]),
                pltpu.make_async_copy(values_ref.at[part], values_buf.at[h], sems.at[h, 1]),
            ]
        )
        for copy in copies[h]:
            copy.start()
    blocks, rows, _ = out_ref.shape
    for h in range(2):
        for copy in copies[h]:
            copy.wait()
        z = keys_buf[h].astype(F32) * values_buf[h].astype(F32)
        z = take(z.T.reshape(blocks, rows, half), order)
        out_ref[:, :, h * half : (h + 1) * half] = z.astype(BF16)


def table_kernel(
    dims, order, place_ref, decay_ref, residue_ref, query_ref,
    high_ref, low_ref, step_ref, grow_ref, inside_ref, whole_ref, cross_ref,
    conv_high_ref, conv_low_ref, after_ref, query_out_ref, sem,
):
    fetch = pltpu.make_async_copy(query_ref, query_out_ref, sem)
    fetch.start()
    blocks, groups, size, length, modes = dims
    decay = decay_ref[...]
    lanes = decay.shape[1]
    row = lax.broadcasted_iota(jnp.int32, (length, length), 0)
    col = lax.broadcasted_iota(jnp.int32, (length, length), 1)
    position = lax.broadcasted_iota(jnp.int32, (length, lanes), 0).astype(F32)
    first = lax.broadcasted_iota(jnp.int32, (length, lanes), 1) < modes
    shape = (blocks, size, lanes)
    block = lax.broadcasted_iota(jnp.int32, shape, 0)
    for g in range(groups):
        rate = decay[g : g + 1]
        high, low = split(jnp.exp(-rate * ((length - 1) - position)))
        high_ref[g] = high
        low_ref[g] = low
        grow = jnp.exp(-rate[None] * (block * length).astype(F32))
        grow_ref[:, g] = jnp.where(own_lanes(shape, modes), grow, 0.0)
        amplitude = residue_ref[g : g + 1] * jnp.sqrt(2.0 * rate)
        rise = jnp.where(first, jnp.exp(rate * position), 0.0)
        fall = amplitude * jnp.exp(-rate * position)
        high, low = split(jnp.where(row <= col, dot_nt(rise, fall), 0.0))
        conv_high_ref[g] = high
        conv_low_ref[g] = low
        after_ref[g] = amplitude * jnp.exp(-rate * (position + 1.0))
    step_ref[...] = jnp.exp(-decay * float(length))
    shape = inside_ref.shape
    span = blocks * length
    place = place_ref[0]
    index = lax.broadcasted_iota(jnp.int32, shape, 0)
    gap = place - 1 - index
    away = jnp.maximum(gap, 0) * span
    inside = jnp.where(gap >= 0, jnp.exp(-decay[None] * away.astype(F32)), 0.0)
    inside_ref[...] = take(inside, order)
    left = (shape[0] - 1 - index) * span
    whole_ref[...] = take(jnp.exp(-decay[None] * left.astype(F32)), order)
    cross_ref[...] = jnp.exp(-decay * (place * span).astype(F32))
    fetch.wait()


def block_kernel(
    dims, order, z_ref, high_ref, low_ref, step_ref, conv_high_ref, conv_low_ref, after_ref, skip_ref,
    end_ref, out_ref, state_ref,
):
    blocks, groups, size, length, modes = dims
    lanes = step_ref.shape[1]
    z = take(z_ref[...].astype(F32), inverse(order))
    skipped = (skip_ref[...][None] * z).reshape(blocks, groups, size, length)
    z = z.reshape(blocks, groups, size, length)
    mine = own_lanes((size, lanes), modes)
    packed = []
    for g in range(groups):
        rows = z[:, g].reshape(blocks * size, length).astype(BF16)
        ends = (dot(rows, high_ref[g]) + dot(rows, low_ref[g])).reshape(blocks, size, lanes)
        step = step_ref[g : g + 1]
        state = jnp.zeros((size, lanes), F32)
        for b in range(blocks):
            state_ref[b] = state
            state = state * step + jnp.where(mine, ends[b], 0.0)
        packed.append(jnp.sum(state, axis=0, keepdims=True))
        conv = dot(rows, conv_high_ref[g]) + dot(rows, conv_low_ref[g])
        carried = dot_nt(state_ref[...].reshape(blocks * size, lanes), after_ref[g])
        out_ref[:, g] = (conv + carried).reshape(blocks, size, length) + skipped[:, g]
    packed = jnp.concatenate(packed, axis=0)
    end_ref[...] = jnp.broadcast_to(packed[None], end_ref.shape)


def total_kernel(ends_ref, whole_ref, total_ref):
    total_ref[...] = jnp.sum(ends_ref[...] * whole_ref[...], axis=0)


def add_carried(dims, order, enter, grow_ref, after_ref, local_ref, out_ref):
    blocks, groups, size, length, modes = dims
    lanes = enter.shape[1]
    mixed = []
    for g in range(groups):
        state = (grow_ref[:, g] * enter[g : g + 1][None]).reshape(blocks * size, lanes)
        carried = dot_nt(state, after_ref[g]).reshape(blocks, size, length)
        mixed.append(local_ref[:, g] + carried)
    mixed = jnp.stack(mixed, axis=1).reshape(blocks, groups * size, length)
    out_ref[...] = take(mixed, order).astype(BF16)


def carry_first_kernel(dims, order, ends_ref, inside_ref, *refs):
    add_carried(dims, order, jnp.sum(ends_ref[...] * inside_ref[...], axis=0), *refs)


def carry_second_kernel(dims, order, ends_ref, inside_ref, before_ref, cross_ref, *refs):
    enter = jnp.sum(ends_ref[...] * inside_ref[...], axis=0)
    add_carried(dims, order, enter + before_ref[...] * cross_ref[...], *refs)


def gate_out_kernel(order, query_ref, mixed_ref, out_ref):
    chan, length = out_ref.shape[1], out_ref.shape[0]
    mixed = take(mixed_ref[...].astype(F32), inverse(order)).reshape(chan, length).T
    out_ref[...] = (query_ref[...].astype(F32) * mixed).astype(BF16)


def on_device(query, keys, values, decay, residue, skip):
    seq_count = lax.axis_size("yc")
    blocks = lax.axis_size("chan")
    length, chan = query.shape
    rows = skip.shape[0]
    groups, modes = decay.shape
    size = rows // groups
    lanes = size * modes
    dims = (blocks, groups, size, length, modes)
    shape = jax.ShapeDtypeStruct
    whole = length * chan

    decay_row = jnp.tile(decay, (1, size))
    residue_row = jnp.tile(residue, (1, size))
    skip_col = skip.reshape(rows, 1)
    place = lax.axis_index("yc").astype(jnp.int32).reshape(1)

    def exchange(axis, order):
        return lambda a: lax.all_to_all(
            a, axis, 0, 0, tiled=True, axis_index_groups=[list(order)]
        )

    gated = call(
        functools.partial(gate_in_kernel, TOKENS_IN), shape((blocks, rows, length), BF16),
        [HBM] * 2, whole, 6 * whole, 60,
        scratch_shapes=[
            pltpu.VMEM((2, length // 2, chan), BF16),
            pltpu.VMEM((2, length // 2, chan), BF16),
            pltpu.SemaphoreType.DMA((2, 2)),
        ],
    )(keys, values)
    z = exchange("chan", TOKENS_IN)(gated)
    table = shape((groups, length, lanes), BF16)
    conv_table = shape((groups, length, length), BF16)
    weights = shape((seq_count, groups, lanes), F32)
    vector = shape((groups, lanes), F32)
    high, low, step, grow, inside, total_w, cross, conv_high, conv_low, after, query_in = call(
        functools.partial(table_kernel, dims, STATES),
        (
            table, table, vector, shape((blocks, groups, size, lanes), F32),
            weights, weights, vector,
            conv_table, conv_table, shape((groups, length, lanes), F32),
            shape((length, chan), BF16),
        ),
        [SMEM, VMEM, VMEM, HBM], 100 * whole, 16 * whole,
        scratch_shapes=[pltpu.SemaphoreType.DMA],
    )(place, decay_row, residue_row, query)
    ends, local = call(
        functools.partial(block_kernel, dims, TOKENS_IN),
        (weights, shape((blocks, groups, size, length), F32)),
        [VMEM] * 8, 8 * length * whole, 16 * whole,
        scratch_shapes=[pltpu.VMEM((blocks, size, lanes), F32)],
    )(z, high, low, step, conv_high, conv_low, after, skip_col)

    half = lax.axis_index("zh")
    ends = lax.cond(half == 0, exchange("yc", STATES), lambda a: a, ends)
    total = call(total_kernel, vector, [VMEM] * 2, whole, whole)(ends, total_w)
    before = lax.ppermute(total, "zh", [(0, 1)])

    def finish(kernel, args):
        mixed = call(
            functools.partial(kernel, dims, TOKENS_OUT), shape((blocks, rows, length), BF16),
            [VMEM] * (len(args) + 3), 12 * lanes * whole, 8 * whole,
        )(*args, grow, after, local)
        return exchange("chan", TOKENS_OUT)(mixed)

    def first_half(ends, mixed):
        return ends, finish(carry_first_kernel, (ends, inside))

    def second_half(ends, mixed):
        return exchange("yc", STATES)(ends), mixed

    def second_finish(mixed, before):
        return finish(carry_second_kernel, (ends, inside, before, cross))

    ends, mixed = lax.cond(half == 0, first_half, second_half, ends, z)
    mixed = lax.cond(half == 1, second_finish, lambda mixed, before: mixed, mixed, before)
    return call(
        functools.partial(gate_out_kernel, TOKENS_OUT), shape((length, chan), BF16),
        [VMEM] * 2, whole, 6 * whole,
    )(query_in, mixed)


def solution(mesh):
    chan = mesh.shape["chan"]
    cut = Mesh(mesh.devices.reshape(HALVES, -1, chan), ("zh", "yc", "chan"))
    tokens = P(("zh", "yc", "chan"), None)
    return jax.shard_map(
        on_device,
        mesh=cut,
        in_specs=(tokens, tokens, tokens, P("chan", None), P("chan", None), P("chan")),
        out_specs=tokens,
        check_vma=False,
    )
```

```python
import functools

import jax
import jax.numpy as jnp
from jax import lax
from jax.experimental import pallas as pl
from jax.experimental.pallas import tpu as pltpu
from jax.sharding import Mesh
from jax.sharding import PartitionSpec as P

F32 = jnp.float32
BF16 = jnp.bfloat16
VMEM = pl.BlockSpec(memory_space=pltpu.VMEM)
SMEM = pl.BlockSpec(memory_space=pltpu.SMEM)
HBM = pl.BlockSpec(memory_space=pltpu.HBM)
NT = (((1,), (1,)), ((), ()))
HALVES = 2

TOKENS_IN = [10, 13, 2, 4, 0, 14, 3, 5, 1, 8, 15, 6, 9, 7, 12, 11]
STATES = [9, 8, 7, 13, 4, 0, 14, 12, 1, 3, 10, 11, 5, 6, 15, 2]
TOKENS_OUT = [10, 11, 12, 0, 4, 3, 13, 2, 1, 7, 9, 15, 8, 14, 5, 6]


def call(body, out_shape, in_specs, flops, nbytes, vmem=16, **kw):
    return pl.pallas_call(
        body,
        out_shape=out_shape,
        in_specs=in_specs,
        out_specs=jax.tree.map(lambda _: VMEM, out_shape),
        cost_estimate=pl.CostEstimate(flops=flops, bytes_accessed=nbytes, transcendentals=0),
        compiler_params=pltpu.CompilerParams(vmem_limit_bytes=vmem << 20),
        **kw,
    )


def split(table):
    high = table.astype(BF16)
    return high, (table - high.astype(F32)).astype(BF16)


def dot(a, b):
    return jnp.dot(a, b, preferred_element_type=F32)


def dot_nt(a, b):
    return lax.dot_general(
        a, b, NT, precision=lax.Precision.HIGHEST, preferred_element_type=F32
    )


def dot_nt_split(a, high, low):
    a_high, a_low = split(a)
    one = functools.partial(lax.dot_general, dimension_numbers=NT, preferred_element_type=F32)
    return one(a_high, high) + (one(a_high, low) + one(a_low, high))


def own_lanes(shape, modes):
    row = lax.broadcasted_iota(jnp.int32, shape, len(shape) - 2)
    lane = lax.broadcasted_iota(jnp.int32, shape, len(shape) - 1)
    return row == lane // modes


def take(data, order):
    return jnp.stack([data[i] for i in order], axis=0)


def inverse(order):
    return [order.index(i) for i in range(len(order))]


def gate_in_kernel(order, keys_ref, values_ref, out_ref, keys_buf, values_buf, sems):
    half = keys_buf.shape[1]
    copies = []
    for h in range(2):
        part = pl.ds(h * half, half)
        copies.append(
            [
                pltpu.make_async_copy(keys_ref.at[part], keys_buf.at[h], sems.at[h, 0]),
                pltpu.make_async_copy(values_ref.at[part], values_buf.at[h], sems.at[h, 1]),
            ]
        )
        for copy in copies[h]:
            copy.start()
    blocks, rows, _ = out_ref.shape
    for h in range(2):
        for copy in copies[h]:
            copy.wait()
        z = keys_buf[h].astype(F32) * values_buf[h].astype(F32)
        z = z.astype(BF16).T.reshape(blocks, rows, half)
        out_ref[:, :, h * half : (h + 1) * half] = take(z, order)


def table_kernel(
    dims, order, place_ref, decay_ref, residue_ref, query_ref,
    high_ref, low_ref, step_ref, grow_ref, inside_ref, whole_ref, cross_ref,
    conv_high_ref, conv_low_ref, after_ref, query_out_ref, sem,
):
    fetch = pltpu.make_async_copy(query_ref, query_out_ref, sem)
    fetch.start()
    blocks, groups, size, length, modes = dims
    decay = decay_ref[...]
    lanes = decay.shape[1]
    row = lax.broadcasted_iota(jnp.int32, (length, length), 0)
    col = lax.broadcasted_iota(jnp.int32, (length, length), 1)
    position = lax.broadcasted_iota(jnp.int32, (length, lanes), 0).astype(F32)
    first = lax.broadcasted_iota(jnp.int32, (length, lanes), 1) < modes
    shape = (blocks, size, lanes)
    block = lax.broadcasted_iota(jnp.int32, shape, 0)
    for g in range(groups):
        rate = decay[g : g + 1]
        high, low = split(jnp.exp(-rate * ((length - 1) - position)))
        high_ref[g] = high
        low_ref[g] = low
        grow = jnp.exp(-rate[None] * (block * length).astype(F32))
        grow_ref[:, g] = jnp.where(own_lanes(shape, modes), grow, 0.0)
        amplitude = residue_ref[g : g + 1] * jnp.sqrt(2.0 * rate)
        rise = jnp.where(first, jnp.exp(rate * position), 0.0)
        fall = amplitude * jnp.exp(-rate * position)
        high, low = split(jnp.where(row <= col, dot_nt(rise, fall), 0.0))
        conv_high_ref[g] = high
        conv_low_ref[g] = low
        high, low = split(amplitude * jnp.exp(-rate * (position + 1.0)))
        after_ref[0, g] = high
        after_ref[1, g] = low
    step_ref[...] = jnp.exp(-decay * float(length))
    shape = inside_ref.shape
    span = blocks * length
    place = place_ref[0]
    index = lax.broadcasted_iota(jnp.int32, shape, 0)
    gap = place - 1 - index
    away = jnp.maximum(gap, 0) * span
    inside = jnp.where(gap >= 0, jnp.exp(-decay[None] * away.astype(F32)), 0.0)
    inside_ref[...] = take(inside, order)
    left = (shape[0] - 1 - index) * span
    whole_ref[...] = take(jnp.exp(-decay[None] * left.astype(F32)), order)
    cross_ref[...] = jnp.exp(-decay * (place * span).astype(F32))
    fetch.wait()


def block_kernel(
    dims, order, z_ref, high_ref, low_ref, step_ref, conv_high_ref, conv_low_ref, after_ref, skip_ref,
    end_ref, out_ref, state_ref,
):
    blocks, groups, size, length, modes = dims
    lanes = step_ref.shape[1]
    z = take(z_ref[...].astype(F32), inverse(order))
    skipped = (skip_ref[...][None] * z).reshape(blocks, groups, size, length)
    z = z.reshape(blocks, groups, size, length)
    mine = own_lanes((size, lanes), modes)
    packed = []
    for g in range(groups):
        rows = z[:, g].reshape(blocks * size, length).astype(BF16)
        ends = (dot(rows, high_ref[g]) + dot(rows, low_ref[g])).reshape(blocks, size, lanes)
        step = step_ref[g : g + 1]
        state = jnp.zeros((size, lanes), F32)
        for b in range(blocks):
            state_ref[b] = state
            state = state * step + jnp.where(mine, ends[b], 0.0)
        packed.append(jnp.sum(state, axis=0, keepdims=True))
        conv = dot(rows, conv_high_ref[g]) + dot(rows, conv_low_ref[g])
        states = state_ref[...].reshape(blocks * size, lanes)
        carried = dot_nt_split(states, after_ref[0, g], after_ref[1, g])
        out_ref[:, g] = (conv + carried).reshape(blocks, size, length) + skipped[:, g]
    packed = jnp.concatenate(packed, axis=0)
    end_ref[...] = jnp.broadcast_to(packed[None], end_ref.shape)


def total_kernel(ends_ref, whole_ref, total_ref):
    total_ref[...] = jnp.sum(ends_ref[...] * whole_ref[...], axis=0)


def add_carried(dims, order, enter, grow_ref, after_ref, local_ref, out_ref):
    blocks, groups, size, length, modes = dims
    lanes = enter.shape[1]
    mixed = []
    for g in range(groups):
        state = (grow_ref[:, g] * enter[g : g + 1][None]).reshape(blocks * size, lanes)
        carried = dot_nt_split(state, after_ref[0, g], after_ref[1, g])
        carried = carried.reshape(blocks, size, length)
        mixed.append(local_ref[:, g] + carried)
    mixed = jnp.stack(mixed, axis=1).reshape(blocks, groups * size, length)
    out_ref[...] = take(mixed, order).astype(BF16)


def carry_first_kernel(dims, order, ends_ref, inside_ref, *refs):
    add_carried(dims, order, jnp.sum(ends_ref[...] * inside_ref[...], axis=0), *refs)


def carry_second_kernel(dims, order, ends_ref, inside_ref, before_ref, cross_ref, *refs):
    enter = jnp.sum(ends_ref[...] * inside_ref[...], axis=0)
    add_carried(dims, order, enter + before_ref[...] * cross_ref[...], *refs)


def gate_out_kernel(order, query_ref, mixed_ref, out_ref):
    chan, length = out_ref.shape[1], out_ref.shape[0]
    mixed = take(mixed_ref[...], inverse(order)).reshape(chan, length).T
    out_ref[...] = (query_ref[...].astype(F32) * mixed.astype(F32)).astype(BF16)


def on_device(query, keys, values, decay, residue, skip):
    seq_count = lax.axis_size("yc")
    blocks = lax.axis_size("chan")
    length, chan = query.shape
    rows = skip.shape[0]
    groups, modes = decay.shape
    size = rows // groups
    lanes = size * modes
    dims = (blocks, groups, size, length, modes)
    shape = jax.ShapeDtypeStruct
    whole = length * chan

    decay_row = jnp.tile(decay, (1, size))
    residue_row = jnp.tile(residue, (1, size))
    skip_col = skip.reshape(rows, 1)
    place = lax.axis_index("yc").astype(jnp.int32).reshape(1)

    def exchange(axis, order):
        return lambda a: lax.all_to_all(
            a, axis, 0, 0, tiled=True, axis_index_groups=[list(order)]
        )

    gated = call(
        functools.partial(gate_in_kernel, TOKENS_IN), shape((blocks, rows, length), BF16),
        [HBM] * 2, whole, 6 * whole, 60,
        scratch_shapes=[
            pltpu.VMEM((2, length // 2, chan), BF16),
            pltpu.VMEM((2, length // 2, chan), BF16),
            pltpu.SemaphoreType.DMA((2, 2)),
        ],
    )(keys, values)
    z = exchange("chan", TOKENS_IN)(gated)
    table = shape((groups, length, lanes), BF16)
    conv_table = shape((groups, length, length), BF16)
    weights = shape((seq_count, groups, lanes), F32)
    vector = shape((groups, lanes), F32)
    high, low, step, grow, inside, total_w, cross, conv_high, conv_low, after, query_in = call(
        functools.partial(table_kernel, dims, STATES),
        (
            table, table, vector, shape((blocks, groups, size, lanes), F32),
            weights, weights, vector,
            conv_table, conv_table, shape((2, groups, length, lanes), BF16),
            shape((length, chan), BF16),
        ),
        [SMEM, VMEM, VMEM, HBM], 100 * whole, 16 * whole,
        scratch_shapes=[pltpu.SemaphoreType.DMA],
    )(place, decay_row, residue_row, query)
    ends, local = call(
        functools.partial(block_kernel, dims, TOKENS_IN),
        (weights, shape((blocks, groups, size, length), F32)),
        [VMEM] * 8, 8 * length * whole, 16 * whole,
        scratch_shapes=[pltpu.VMEM((blocks, size, lanes), F32)],
    )(z, high, low, step, conv_high, conv_low, after, skip_col)

    half = lax.axis_index("zh")
    ends = lax.cond(half == 0, exchange("yc", STATES), lambda a: a, ends)
    total = call(total_kernel, vector, [VMEM] * 2, whole, whole)(ends, total_w)
    before = lax.ppermute(total, "zh", [(0, 1)])

    def finish(kernel, args):
        mixed = call(
            functools.partial(kernel, dims, TOKENS_OUT), shape((blocks, rows, length), BF16),
            [VMEM] * (len(args) + 3), 12 * lanes * whole, 8 * whole,
        )(*args, grow, after, local)
        return exchange("chan", TOKENS_OUT)(mixed)

    def first_half(ends, mixed):
        return ends, finish(carry_first_kernel, (ends, inside))

    def second_half(ends, mixed):
        return exchange("yc", STATES)(ends), mixed

    def second_finish(mixed, before):
        return finish(carry_second_kernel, (ends, inside, before, cross))

    ends, mixed = lax.cond(half == 0, first_half, second_half, ends, z)
    mixed = lax.cond(half == 1, second_finish, lambda mixed, before: mixed, mixed, before)
    return call(
        functools.partial(gate_out_kernel, TOKENS_OUT), shape((length, chan), BF16),
        [VMEM] * 2, whole, 6 * whole,
    )(query_in, mixed)


def solution(mesh):
    chan = mesh.shape["chan"]
    cut = Mesh(mesh.devices.reshape(HALVES, -1, chan), ("zh", "yc", "chan"))
    tokens = P(("zh", "yc", "chan"), None)
    return jax.shard_map(
        on_device,
        mesh=cut,
        in_specs=(tokens, tokens, tokens, P("chan", None), P("chan", None), P("chan")),
        out_specs=tokens,
        check_vma=False,
    )
```

```python
import functools

import jax
import jax.numpy as jnp
from jax import lax
from jax.experimental import pallas as pl
from jax.experimental.pallas import tpu as pltpu
from jax.sharding import Mesh
from jax.sharding import PartitionSpec as P

F32 = jnp.float32
BF16 = jnp.bfloat16
VMEM = pl.BlockSpec(memory_space=pltpu.VMEM)
SMEM = pl.BlockSpec(memory_space=pltpu.SMEM)
HBM = pl.BlockSpec(memory_space=pltpu.HBM)
NT = (((1,), (1,)), ((), ()))
HALVES = 2

TOKENS_IN = [10, 13, 2, 4, 0, 14, 3, 5, 1, 8, 15, 6, 9, 7, 12, 11]
STATES = [9, 8, 7, 13, 4, 0, 14, 12, 1, 3, 10, 11, 5, 6, 15, 2]
TOKENS_OUT = [10, 11, 12, 0, 4, 3, 13, 2, 1, 7, 9, 15, 8, 14, 5, 6]


def call(body, out_shape, in_specs, flops, nbytes, vmem=16, **kw):
    return pl.pallas_call(
        body,
        out_shape=out_shape,
        in_specs=in_specs,
        out_specs=jax.tree.map(lambda _: VMEM, out_shape),
        cost_estimate=pl.CostEstimate(flops=flops, bytes_accessed=nbytes, transcendentals=0),
        compiler_params=pltpu.CompilerParams(vmem_limit_bytes=vmem << 20),
        **kw,
    )


def split(table):
    high = table.astype(BF16)
    return high, (table - high.astype(F32)).astype(BF16)


def dot(a, b):
    return jnp.dot(a, b, preferred_element_type=F32)


def dot_nt(a, b):
    return lax.dot_general(
        a, b, NT, precision=lax.Precision.HIGHEST, preferred_element_type=F32
    )


def dot_nt_split(a, high, low):
    a_high, a_low = split(a)
    one = functools.partial(lax.dot_general, dimension_numbers=NT, preferred_element_type=F32)
    both = one(jnp.concatenate([a_high, a_low], axis=1), jnp.concatenate([high, high], axis=1))
    return both + one(a_high, low)


def own_lanes(shape, modes):
    row = lax.broadcasted_iota(jnp.int32, shape, len(shape) - 2)
    lane = lax.broadcasted_iota(jnp.int32, shape, len(shape) - 1)
    return row == lane // modes


def take(data, order):
    return jnp.stack([data[i] for i in order], axis=0)


def inverse(order):
    return [order.index(i) for i in range(len(order))]


def gate_in_kernel(order, keys_ref, values_ref, out_ref, keys_buf, values_buf, sems):
    half = keys_buf.shape[1]
    copies = []
    for h in range(2):
        part = pl.ds(h * half, half)
        copies.append(
            [
                pltpu.make_async_copy(keys_ref.at[part], keys_buf.at[h], sems.at[h, 0]),
                pltpu.make_async_copy(values_ref.at[part], values_buf.at[h], sems.at[h, 1]),
            ]
        )
        for copy in copies[h]:
            copy.start()
    blocks, rows, _ = out_ref.shape
    for h in range(2):
        for copy in copies[h]:
            copy.wait()
        z = keys_buf[h].astype(F32) * values_buf[h].astype(F32)
        z = z.astype(BF16).T.reshape(blocks, rows, half)
        out_ref[:, :, h * half : (h + 1) * half] = take(z, order)


def table_kernel(
    dims, order, place_ref, decay_ref, residue_ref, query_ref,
    high_ref, low_ref, step_ref, grow_ref, inside_ref, whole_ref, cross_ref,
    conv_high_ref, conv_low_ref, after_ref, query_out_ref, sem,
):
    fetch = pltpu.make_async_copy(query_ref, query_out_ref, sem)
    fetch.start()
    blocks, groups, size, length, modes = dims
    decay = decay_ref[...]
    lanes = decay.shape[1]
    row = lax.broadcasted_iota(jnp.int32, (length, length), 0)
    col = lax.broadcasted_iota(jnp.int32, (length, length), 1)
    position = lax.broadcasted_iota(jnp.int32, (length, lanes), 0).astype(F32)
    first = lax.broadcasted_iota(jnp.int32, (length, lanes), 1) < modes
    shape = (blocks, size, lanes)
    block = lax.broadcasted_iota(jnp.int32, shape, 0)
    for g in range(groups):
        rate = decay[g : g + 1]
        high, low = split(jnp.exp(-rate * ((length - 1) - position)))
        high_ref[g] = high
        low_ref[g] = low
        grow = jnp.exp(-rate[None] * (block * length).astype(F32))
        grow_ref[:, g] = jnp.where(own_lanes(shape, modes), grow, 0.0)
        amplitude = residue_ref[g : g + 1] * jnp.sqrt(2.0 * rate)
        rise = jnp.where(first, jnp.exp(rate * position), 0.0)
        fall = amplitude * jnp.exp(-rate * position)
        high, low = split(jnp.where(row <= col, dot_nt(rise, fall), 0.0))
        conv_high_ref[g] = high
        conv_low_ref[g] = low
        high, low = split(amplitude * jnp.exp(-rate * (position + 1.0)))
        after_ref[0, g] = high
        after_ref[1, g] = low
    step_ref[...] = jnp.exp(-decay * float(length))
    shape = inside_ref.shape
    span = blocks * length
    place = place_ref[0]
    index = lax.broadcasted_iota(jnp.int32, shape, 0)
    gap = place - 1 - index
    away = jnp.maximum(gap, 0) * span
    inside = jnp.where(gap >= 0, jnp.exp(-decay[None] * away.astype(F32)), 0.0)
    inside_ref[...] = take(inside, order)
    left = (shape[0] - 1 - index) * span
    whole_ref[...] = take(jnp.exp(-decay[None] * left.astype(F32)), order)
    cross_ref[...] = jnp.exp(-decay * (place * span).astype(F32))
    fetch.wait()


def block_kernel(
    dims, order, z_ref, high_ref, low_ref, step_ref, conv_high_ref, conv_low_ref, after_ref, skip_ref,
    end_ref, out_ref, state_ref,
):
    blocks, groups, size, length, modes = dims
    lanes = step_ref.shape[1]
    z = take(z_ref[...].astype(F32), inverse(order))
    skipped = (skip_ref[...][None] * z).reshape(blocks, groups, size, length)
    z = z.reshape(blocks, groups, size, length)
    mine = own_lanes((size, lanes), modes)
    packed = []
    for g in range(groups):
        rows = z[:, g].reshape(blocks * size, length).astype(BF16)
        ends = dot(rows, jnp.concatenate([high_ref[g], low_ref[g]], axis=1))
        ends = (ends[:, :lanes] + ends[:, lanes:]).reshape(blocks, size, lanes)
        step = step_ref[g : g + 1]
        state = jnp.zeros((size, lanes), F32)
        for b in range(blocks):
            state_ref[b] = state
            state = state * step + jnp.where(mine, ends[b], 0.0)
        packed.append(jnp.sum(state, axis=0, keepdims=True))
        conv = dot(rows, conv_high_ref[g]) + dot(rows, conv_low_ref[g])
        states = state_ref[...].reshape(blocks * size, lanes)
        carried = dot_nt_split(states, after_ref[0, g], after_ref[1, g])
        out_ref[:, g] = (conv + carried).reshape(blocks, size, length) + skipped[:, g]
    packed = jnp.concatenate(packed, axis=0)
    end_ref[...] = jnp.broadcast_to(packed[None], end_ref.shape)


def total_kernel(ends_ref, whole_ref, total_ref):
    total_ref[...] = jnp.sum(ends_ref[...] * whole_ref[...], axis=0)


def add_carried(dims, order, enter, grow_ref, after_ref, local_ref, out_ref):
    blocks, groups, size, length, modes = dims
    lanes = enter.shape[1]
    mixed = []
    for g in range(groups):
        state = (grow_ref[:, g] * enter[g : g + 1][None]).reshape(blocks * size, lanes)
        carried = dot_nt_split(state, after_ref[0, g], after_ref[1, g])
        carried = carried.reshape(blocks, size, length)
        mixed.append(local_ref[:, g] + carried)
    mixed = jnp.stack(mixed, axis=1).reshape(blocks, groups * size, length)
    out_ref[...] = take(mixed, order).astype(BF16)


def carry_first_kernel(dims, order, ends_ref, inside_ref, *refs):
    add_carried(dims, order, jnp.sum(ends_ref[...] * inside_ref[...], axis=0), *refs)


def carry_second_kernel(dims, order, ends_ref, inside_ref, before_ref, cross_ref, *refs):
    enter = jnp.sum(ends_ref[...] * inside_ref[...], axis=0)
    add_carried(dims, order, enter + before_ref[...] * cross_ref[...], *refs)


def gate_out_kernel(order, query_ref, mixed_ref, out_ref):
    chan, length = out_ref.shape[1], out_ref.shape[0]
    mixed = take(mixed_ref[...], inverse(order)).reshape(chan, length).T
    out_ref[...] = (query_ref[...].astype(F32) * mixed.astype(F32)).astype(BF16)


def on_device(query, keys, values, decay, residue, skip):
    seq_count = lax.axis_size("yc")
    blocks = lax.axis_size("chan")
    length, chan = query.shape
    rows = skip.shape[0]
    groups, modes = decay.shape
    size = rows // groups
    lanes = size * modes
    dims = (blocks, groups, size, length, modes)
    shape = jax.ShapeDtypeStruct
    whole = length * chan

    decay_row = jnp.tile(decay, (1, size))
    residue_row = jnp.tile(residue, (1, size))
    skip_col = skip.reshape(rows, 1)
    place = lax.axis_index("yc").astype(jnp.int32).reshape(1)

    def exchange(axis, order):
        return lambda a: lax.all_to_all(
            a, axis, 0, 0, tiled=True, axis_index_groups=[list(order)]
        )

    gated = call(
        functools.partial(gate_in_kernel, TOKENS_IN), shape((blocks, rows, length), BF16),
        [HBM] * 2, whole, 6 * whole, 60,
        scratch_shapes=[
            pltpu.VMEM((2, length // 2, chan), BF16),
            pltpu.VMEM((2, length // 2, chan), BF16),
            pltpu.SemaphoreType.DMA((2, 2)),
        ],
    )(keys, values)
    z = exchange("chan", TOKENS_IN)(gated)
    table = shape((groups, length, lanes), BF16)
    conv_table = shape((groups, length, length), BF16)
    weights = shape((seq_count, groups, lanes), F32)
    vector = shape((groups, lanes), F32)
    high, low, step, grow, inside, total_w, cross, conv_high, conv_low, after, query_in = call(
        functools.partial(table_kernel, dims, STATES),
        (
            table, table, vector, shape((blocks, groups, size, lanes), F32),
            weights, weights, vector,
            conv_table, conv_table, shape((2, groups, length, lanes), BF16),
            shape((length, chan), BF16),
        ),
        [SMEM, VMEM, VMEM, HBM], 100 * whole, 16 * whole,
        scratch_shapes=[pltpu.SemaphoreType.DMA],
    )(place, decay_row, residue_row, query)
    ends, local = call(
        functools.partial(block_kernel, dims, TOKENS_IN),
        (weights, shape((blocks, groups, size, length), F32)),
        [VMEM] * 8, 8 * length * whole, 16 * whole,
        scratch_shapes=[pltpu.VMEM((blocks, size, lanes), F32)],
    )(z, high, low, step, conv_high, conv_low, after, skip_col)

    half = lax.axis_index("zh")
    ends = lax.cond(half == 0, exchange("yc", STATES), lambda a: a, ends)
    total = call(total_kernel, vector, [VMEM] * 2, whole, whole)(ends, total_w)
    before = lax.ppermute(total, "zh", [(0, 1)])

    def finish(kernel, args):
        mixed = call(
            functools.partial(kernel, dims, TOKENS_OUT), shape((blocks, rows, length), BF16),
            [VMEM] * (len(args) + 3), 12 * lanes * whole, 8 * whole,
        )(*args, grow, after, local)
        return exchange("chan", TOKENS_OUT)(mixed)

    def first_half(ends, mixed):
        return ends, finish(carry_first_kernel, (ends, inside))

    def second_half(ends, mixed):
        return exchange("yc", STATES)(ends), mixed

    def second_finish(mixed, before):
        return finish(carry_second_kernel, (ends, inside, before, cross))

    ends, mixed = lax.cond(half == 0, first_half, second_half, ends, z)
    mixed = lax.cond(half == 1, second_finish, lambda mixed, before: mixed, mixed, before)
    return call(
        functools.partial(gate_out_kernel, TOKENS_OUT), shape((length, chan), BF16),
        [VMEM] * 2, whole, 6 * whole,
    )(query_in, mixed)


def solution(mesh):
    chan = mesh.shape["chan"]
    cut = Mesh(mesh.devices.reshape(HALVES, -1, chan), ("zh", "yc", "chan"))
    tokens = P(("zh", "yc", "chan"), None)
    return jax.shard_map(
        on_device,
        mesh=cut,
        in_specs=(tokens, tokens, tokens, P("chan", None), P("chan", None), P("chan")),
        out_specs=tokens,
        check_vma=False,
    )
```

```python
import functools

import jax
import jax.numpy as jnp
from jax import lax
from jax.experimental import pallas as pl
from jax.experimental.pallas import tpu as pltpu
from jax.sharding import Mesh
from jax.sharding import PartitionSpec as P

F32 = jnp.float32
BF16 = jnp.bfloat16
VMEM = pl.BlockSpec(memory_space=pltpu.VMEM)
SMEM = pl.BlockSpec(memory_space=pltpu.SMEM)
HBM = pl.BlockSpec(memory_space=pltpu.HBM)
NT = (((1,), (1,)), ((), ()))
HALVES = 2

TOKENS_IN = [10, 13, 2, 4, 0, 14, 3, 5, 1, 8, 15, 6, 9, 7, 12, 11]
STATES = [9, 8, 7, 13, 4, 0, 14, 12, 1, 3, 10, 11, 5, 6, 15, 2]
TOKENS_OUT = [10, 11, 12, 0, 4, 3, 13, 2, 1, 7, 9, 15, 8, 14, 5, 6]


def call(body, out_shape, in_specs, flops, nbytes, vmem=16, **kw):
    return pl.pallas_call(
        body,
        out_shape=out_shape,
        in_specs=in_specs,
        out_specs=jax.tree.map(lambda _: VMEM, out_shape),
        cost_estimate=pl.CostEstimate(flops=flops, bytes_accessed=nbytes, transcendentals=0),
        compiler_params=pltpu.CompilerParams(vmem_limit_bytes=vmem << 20),
        **kw,
    )


def split(table):
    high = table.astype(BF16)
    return high, (table - high.astype(F32)).astype(BF16)


def dot(a, b):
    return jnp.dot(a, b, preferred_element_type=F32)


def dot_nt(a, b):
    return lax.dot_general(
        a, b, NT, precision=lax.Precision.HIGHEST, preferred_element_type=F32
    )


def dot_nt_split(a, high, low):
    a_high, a_low = split(a)
    one = functools.partial(lax.dot_general, dimension_numbers=NT, preferred_element_type=F32)
    both = one(jnp.concatenate([a_high, a_low], axis=1), jnp.concatenate([high, high], axis=1))
    return both + one(a_high, low)


def own_lanes(shape, modes):
    row = lax.broadcasted_iota(jnp.int32, shape, len(shape) - 2)
    lane = lax.broadcasted_iota(jnp.int32, shape, len(shape) - 1)
    return row == lane // modes


def take(data, order):
    return jnp.stack([data[i] for i in order], axis=0)


def inverse(order):
    return [order.index(i) for i in range(len(order))]


def gate_in_kernel(order, keys_ref, values_ref, out_ref, keys_buf, values_buf, sems):
    half = keys_buf.shape[1]
    copies = []
    for h in range(2):
        part = pl.ds(h * half, half)
        copies.append(
            [
                pltpu.make_async_copy(keys_ref.at[part], keys_buf.at[h], sems.at[h, 0]),
                pltpu.make_async_copy(values_ref.at[part], values_buf.at[h], sems.at[h, 1]),
            ]
        )
        for copy in copies[h]:
            copy.start()
    blocks, rows, _ = out_ref.shape
    for h in range(2):
        for copy in copies[h]:
            copy.wait()
        z = keys_buf[h].astype(F32) * values_buf[h].astype(F32)
        z = z.astype(BF16).T.reshape(blocks, rows, half)
        out_ref[:, :, h * half : (h + 1) * half] = take(z, order)


def table_kernel(
    dims, order, place_ref, decay_ref, residue_ref, query_ref,
    high_ref, low_ref, step_ref, grow_ref, inside_ref, whole_ref, cross_ref,
    conv_high_ref, conv_low_ref, after_ref, query_out_ref, sem,
):
    fetch = pltpu.make_async_copy(query_ref, query_out_ref, sem)
    fetch.start()
    blocks, groups, size, length, modes = dims
    decay = decay_ref[...]
    lanes = decay.shape[1]
    row = lax.broadcasted_iota(jnp.int32, (length, length), 0)
    col = lax.broadcasted_iota(jnp.int32, (length, length), 1)
    position = lax.broadcasted_iota(jnp.int32, (length, lanes), 0).astype(F32)
    first = lax.broadcasted_iota(jnp.int32, (length, lanes), 1) < modes
    shape = (blocks, size, lanes)
    block = lax.broadcasted_iota(jnp.int32, shape, 0)
    for g in range(groups):
        rate = decay[g : g + 1]
        high, low = split(jnp.exp(-rate * ((length - 1) - position)))
        high_ref[g] = high
        low_ref[g] = low
        grow = jnp.exp(-rate[None] * (block * length).astype(F32))
        grow_ref[:, g] = jnp.where(own_lanes(shape, modes), grow, 0.0)
        amplitude = residue_ref[g : g + 1] * jnp.sqrt(2.0 * rate)
        rise = jnp.where(first, jnp.exp(rate * position), 0.0)
        fall = amplitude * jnp.exp(-rate * position)
        high, low = split(jnp.where(row <= col, dot_nt(rise, fall), 0.0))
        conv_high_ref[g] = high
        conv_low_ref[g] = low
        high, low = split(amplitude * jnp.exp(-rate * (position + 1.0)))
        after_ref[0, g] = high
        after_ref[1, g] = low
    step_ref[...] = jnp.exp(-decay * float(length))
    shape = inside_ref.shape
    span = blocks * length
    place = place_ref[0]
    index = lax.broadcasted_iota(jnp.int32, shape, 0)
    gap = place - 1 - index
    away = jnp.maximum(gap, 0) * span
    inside = jnp.where(gap >= 0, jnp.exp(-decay[None] * away.astype(F32)), 0.0)
    inside_ref[...] = take(inside, order)
    left = (shape[0] - 1 - index) * span
    whole_ref[...] = take(jnp.exp(-decay[None] * left.astype(F32)), order)
    cross_ref[...] = jnp.exp(-decay * (place * span).astype(F32))
    fetch.wait()


def block_kernel(
    dims, order, z_ref, high_ref, low_ref, step_ref, conv_high_ref, conv_low_ref, after_ref, skip_ref,
    end_ref, out_ref, state_ref,
):
    blocks, groups, size, length, modes = dims
    lanes = step_ref.shape[1]
    z = take(z_ref[...].astype(F32), inverse(order))
    skipped = (skip_ref[...][None] * z).reshape(blocks, groups, size, length)
    z = z.reshape(blocks, groups, size, length)
    mine = own_lanes((size, lanes), modes)
    packed = []
    for g in range(groups):
        rows = z[:, g].reshape(blocks * size, length).astype(BF16)
        ends = dot(rows, jnp.concatenate([high_ref[g], low_ref[g]], axis=1))
        ends = (ends[:, :lanes] + ends[:, lanes:]).reshape(blocks, size, lanes)
        step = step_ref[g : g + 1]
        state = jnp.zeros((size, lanes), F32)
        for b in range(blocks):
            state_ref[g, b] = state
            state = state * step + jnp.where(mine, ends[b], 0.0)
        packed.append(jnp.sum(state, axis=0, keepdims=True))
        conv = dot(rows, conv_high_ref[g]) + dot(rows, conv_low_ref[g])
        states = state_ref[g].reshape(blocks * size, lanes)
        carried = dot_nt_split(states, after_ref[0, g], after_ref[1, g])
        out_ref[:, g] = (conv + carried).reshape(blocks, size, length) + skipped[:, g]
    packed = jnp.concatenate(packed, axis=0)
    end_ref[...] = jnp.broadcast_to(packed[None], end_ref.shape)


def total_kernel(ends_ref, whole_ref, total_ref):
    total_ref[...] = jnp.sum(ends_ref[...] * whole_ref[...], axis=0)


def add_carried(dims, order, enter, grow_ref, after_ref, local_ref, out_ref):
    blocks, groups, size, length, modes = dims
    lanes = enter.shape[1]
    mixed = []
    for g in range(groups):
        state = (grow_ref[:, g] * enter[g : g + 1][None]).reshape(blocks * size, lanes)
        carried = dot_nt_split(state, after_ref[0, g], after_ref[1, g])
        carried = carried.reshape(blocks, size, length)
        mixed.append(local_ref[:, g] + carried)
    mixed = jnp.stack(mixed, axis=1).reshape(blocks, groups * size, length)
    out_ref[...] = take(mixed, order).astype(BF16)


def carry_first_kernel(dims, order, ends_ref, inside_ref, *refs):
    add_carried(dims, order, jnp.sum(ends_ref[...] * inside_ref[...], axis=0), *refs)


def carry_second_kernel(dims, order, ends_ref, inside_ref, before_ref, cross_ref, *refs):
    enter = jnp.sum(ends_ref[...] * inside_ref[...], axis=0)
    add_carried(dims, order, enter + before_ref[...] * cross_ref[...], *refs)


def gate_out_kernel(order, query_ref, mixed_ref, out_ref):
    chan, length = out_ref.shape[1], out_ref.shape[0]
    mixed = take(mixed_ref[...], inverse(order)).reshape(chan, length).T
    out_ref[...] = (query_ref[...].astype(F32) * mixed.astype(F32)).astype(BF16)


def on_device(query, keys, values, decay, residue, skip):
    seq_count = lax.axis_size("yc")
    blocks = lax.axis_size("chan")
    length, chan = query.shape
    rows = skip.shape[0]
    groups, modes = decay.shape
    size = rows // groups
    lanes = size * modes
    dims = (blocks, groups, size, length, modes)
    shape = jax.ShapeDtypeStruct
    whole = length * chan

    decay_row = jnp.tile(decay, (1, size))
    residue_row = jnp.tile(residue, (1, size))
    skip_col = skip.reshape(rows, 1)
    place = lax.axis_index("yc").astype(jnp.int32).reshape(1)

    def exchange(axis, order):
        return lambda a: lax.all_to_all(
            a, axis, 0, 0, tiled=True, axis_index_groups=[list(order)]
        )

    gated = call(
        functools.partial(gate_in_kernel, TOKENS_IN), shape((blocks, rows, length), BF16),
        [HBM] * 2, whole, 6 * whole, 60,
        scratch_shapes=[
            pltpu.VMEM((2, length // 2, chan), BF16),
            pltpu.VMEM((2, length // 2, chan), BF16),
            pltpu.SemaphoreType.DMA((2, 2)),
        ],
    )(keys, values)
    z = exchange("chan", TOKENS_IN)(gated)
    table = shape((groups, length, lanes), BF16)
    conv_table = shape((groups, length, length), BF16)
    weights = shape((seq_count, groups, lanes), F32)
    vector = shape((groups, lanes), F32)
    high, low, step, grow, inside, total_w, cross, conv_high, conv_low, after, query_in = call(
        functools.partial(table_kernel, dims, STATES),
        (
            table, table, vector, shape((blocks, groups, size, lanes), F32),
            weights, weights, vector,
            conv_table, conv_table, shape((2, groups, length, lanes), BF16),
            shape((length, chan), BF16),
        ),
        [SMEM, VMEM, VMEM, HBM], 100 * whole, 16 * whole,
        scratch_shapes=[pltpu.SemaphoreType.DMA],
    )(place, decay_row, residue_row, query)
    ends, local = call(
        functools.partial(block_kernel, dims, TOKENS_IN),
        (weights, shape((blocks, groups, size, length), F32)),
        [VMEM] * 8, 8 * length * whole, 16 * whole,
        scratch_shapes=[pltpu.VMEM((groups, blocks, size, lanes), F32)],
    )(z, high, low, step, conv_high, conv_low, after, skip_col)

    half = lax.axis_index("zh")
    ends = lax.cond(half == 0, exchange("yc", STATES), lambda a: a, ends)
    total = call(total_kernel, vector, [VMEM] * 2, whole, whole)(ends, total_w)
    before = lax.ppermute(total, "zh", [(0, 1)])

    def finish(kernel, args):
        mixed = call(
            functools.partial(kernel, dims, TOKENS_OUT), shape((blocks, rows, length), BF16),
            [VMEM] * (len(args) + 3), 12 * lanes * whole, 8 * whole,
        )(*args, grow, after, local)
        return exchange("chan", TOKENS_OUT)(mixed)

    def first_half(ends, mixed):
        return ends, finish(carry_first_kernel, (ends, inside))

    def second_half(ends, mixed):
        return exchange("yc", STATES)(ends), mixed

    def second_finish(mixed, before):
        return finish(carry_second_kernel, (ends, inside, before, cross))

    ends, mixed = lax.cond(half == 0, first_half, second_half, ends, z)
    mixed = lax.cond(half == 1, second_finish, lambda mixed, before: mixed, mixed, before)
    return call(
        functools.partial(gate_out_kernel, TOKENS_OUT), shape((length, chan), BF16),
        [VMEM] * 2, whole, 6 * whole,
    )(query_in, mixed)


def solution(mesh):
    chan = mesh.shape["chan"]
    cut = Mesh(mesh.devices.reshape(HALVES, -1, chan), ("zh", "yc", "chan"))
    tokens = P(("zh", "yc", "chan"), None)
    return jax.shard_map(
        on_device,
        mesh=cut,
        in_specs=(tokens, tokens, tokens, P("chan", None), P("chan", None), P("chan")),
        out_specs=tokens,
        check_vma=False,
    )
```

```python
import functools

import jax
import jax.numpy as jnp
from jax import lax
from jax.experimental import pallas as pl
from jax.experimental.pallas import tpu as pltpu
from jax.sharding import Mesh
from jax.sharding import PartitionSpec as P

F32 = jnp.float32
BF16 = jnp.bfloat16
VMEM = pl.BlockSpec(memory_space=pltpu.VMEM)
SMEM = pl.BlockSpec(memory_space=pltpu.SMEM)
HBM = pl.BlockSpec(memory_space=pltpu.HBM)
NT = (((1,), (1,)), ((), ()))
HALVES = 2

TOKENS_IN = [10, 13, 2, 4, 0, 14, 3, 5, 1, 8, 15, 6, 9, 7, 12, 11]
STATES = [9, 8, 7, 13, 4, 0, 14, 12, 1, 3, 10, 11, 5, 6, 15, 2]
TOKENS_OUT = [10, 11, 12, 0, 4, 3, 13, 2, 1, 7, 9, 15, 8, 14, 5, 6]


def call(body, out_shape, in_specs, flops, nbytes, vmem=16, **kw):
    return pl.pallas_call(
        body,
        out_shape=out_shape,
        in_specs=in_specs,
        out_specs=jax.tree.map(lambda _: VMEM, out_shape),
        cost_estimate=pl.CostEstimate(flops=flops, bytes_accessed=nbytes, transcendentals=0),
        compiler_params=pltpu.CompilerParams(vmem_limit_bytes=vmem << 20),
        **kw,
    )


def split(table):
    high = table.astype(BF16)
    return high, (table - high.astype(F32)).astype(BF16)


def dot(a, b):
    return jnp.dot(a, b, preferred_element_type=F32)


def dot_nt(a, b):
    return lax.dot_general(
        a, b, NT, precision=lax.Precision.HIGHEST, preferred_element_type=F32
    )


def dot_nt_split(a, high, low):
    a_high, a_low = split(a)
    one = functools.partial(lax.dot_general, dimension_numbers=NT, preferred_element_type=F32)
    both = one(jnp.concatenate([a_high, a_low], axis=1), jnp.concatenate([high, high], axis=1))
    return both + one(a_high, low)


def own_lanes(shape, modes):
    row = lax.broadcasted_iota(jnp.int32, shape, len(shape) - 2)
    lane = lax.broadcasted_iota(jnp.int32, shape, len(shape) - 1)
    return row == lane // modes


def take(data, order):
    return jnp.stack([data[i] for i in order], axis=0)


def inverse(order):
    return [order.index(i) for i in range(len(order))]


def gate_in_kernel(order, keys_ref, values_ref, out_ref, keys_buf, values_buf, sems):
    half = keys_buf.shape[1]
    copies = []
    for h in range(keys_buf.shape[0]):
        part = pl.ds(h * half, half)
        copies.append(
            [
                pltpu.make_async_copy(keys_ref.at[part], keys_buf.at[h], sems.at[h, 0]),
                pltpu.make_async_copy(values_ref.at[part], values_buf.at[h], sems.at[h, 1]),
            ]
        )
        for copy in copies[h]:
            copy.start()
    blocks, rows, _ = out_ref.shape
    for h in range(keys_buf.shape[0]):
        for copy in copies[h]:
            copy.wait()
        z = keys_buf[h].astype(F32) * values_buf[h].astype(F32)
        z = z.astype(BF16).T.reshape(blocks, rows, half)
        out_ref[:, :, h * half : (h + 1) * half] = take(z, order)


def table_kernel(
    dims, order, place_ref, decay_ref, residue_ref, query_ref,
    high_ref, low_ref, step_ref, grow_ref, inside_ref, whole_ref, cross_ref,
    conv_high_ref, conv_low_ref, after_ref, query_out_ref, sem,
):
    fetch = pltpu.make_async_copy(query_ref, query_out_ref, sem)
    fetch.start()
    blocks, groups, size, length, modes = dims
    decay = decay_ref[...]
    lanes = decay.shape[1]
    row = lax.broadcasted_iota(jnp.int32, (length, length), 0)
    col = lax.broadcasted_iota(jnp.int32, (length, length), 1)
    position = lax.broadcasted_iota(jnp.int32, (length, lanes), 0).astype(F32)
    first = lax.broadcasted_iota(jnp.int32, (length, lanes), 1) < modes
    shape = (blocks, size, lanes)
    block = lax.broadcasted_iota(jnp.int32, shape, 0)
    for g in range(groups):
        rate = decay[g : g + 1]
        high, low = split(jnp.exp(-rate * ((length - 1) - position)))
        high_ref[g] = high
        low_ref[g] = low
        grow = jnp.exp(-rate[None] * (block * length).astype(F32))
        grow_ref[:, g] = jnp.where(own_lanes(shape, modes), grow, 0.0)
        amplitude = residue_ref[g : g + 1] * jnp.sqrt(2.0 * rate)
        rise = jnp.where(first, jnp.exp(rate * position), 0.0)
        fall = amplitude * jnp.exp(-rate * position)
        high, low = split(jnp.where(row <= col, dot_nt(rise, fall), 0.0))
        conv_high_ref[g] = high
        conv_low_ref[g] = low
        high, low = split(amplitude * jnp.exp(-rate * (position + 1.0)))
        after_ref[0, g] = high
        after_ref[1, g] = low
    step_ref[...] = jnp.exp(-decay * float(length))
    shape = inside_ref.shape
    span = blocks * length
    place = place_ref[0]
    index = lax.broadcasted_iota(jnp.int32, shape, 0)
    gap = place - 1 - index
    away = jnp.maximum(gap, 0) * span
    inside = jnp.where(gap >= 0, jnp.exp(-decay[None] * away.astype(F32)), 0.0)
    inside_ref[...] = take(inside, order)
    left = (shape[0] - 1 - index) * span
    whole_ref[...] = take(jnp.exp(-decay[None] * left.astype(F32)), order)
    cross_ref[...] = jnp.exp(-decay * (place * span).astype(F32))
    fetch.wait()


def block_kernel(
    dims, order, z_ref, high_ref, low_ref, step_ref, conv_high_ref, conv_low_ref, after_ref, skip_ref,
    end_ref, out_ref, state_ref,
):
    blocks, groups, size, length, modes = dims
    lanes = step_ref.shape[1]
    z = take(z_ref[...].astype(F32), inverse(order))
    skipped = (skip_ref[...][None] * z).reshape(blocks, groups, size, length)
    z = z.reshape(blocks, groups, size, length)
    mine = own_lanes((size, lanes), modes)
    packed = []
    for g in range(groups):
        rows = z[:, g].reshape(blocks * size, length).astype(BF16)
        ends = dot(rows, jnp.concatenate([high_ref[g], low_ref[g]], axis=1))
        ends = (ends[:, :lanes] + ends[:, lanes:]).reshape(blocks, size, lanes)
        step = step_ref[g : g + 1]
        state = jnp.zeros((size, lanes), F32)
        for b in range(blocks):
            state_ref[b] = state
            state = state * step + jnp.where(mine, ends[b], 0.0)
        packed.append(jnp.sum(state, axis=0, keepdims=True))
        conv = dot(rows, conv_high_ref[g]) + dot(rows, conv_low_ref[g])
        states = state_ref[...].reshape(blocks * size, lanes)
        carried = dot_nt_split(states, after_ref[0, g], after_ref[1, g])
        out_ref[:, g] = (conv + carried).reshape(blocks, size, length) + skipped[:, g]
    packed = jnp.concatenate(packed, axis=0)
    end_ref[...] = jnp.broadcast_to(packed[None], end_ref.shape)


def total_kernel(ends_ref, whole_ref, total_ref):
    total_ref[...] = jnp.sum(ends_ref[...] * whole_ref[...], axis=0)


def add_carried(dims, order, enter, grow_ref, after_ref, local_ref, out_ref):
    blocks, groups, size, length, modes = dims
    lanes = enter.shape[1]
    mixed = []
    for g in range(groups):
        state = (grow_ref[:, g] * enter[g : g + 1][None]).reshape(blocks * size, lanes)
        carried = dot_nt_split(state, after_ref[0, g], after_ref[1, g])
        carried = carried.reshape(blocks, size, length)
        mixed.append(local_ref[:, g] + carried)
    mixed = jnp.stack(mixed, axis=1).reshape(blocks, groups * size, length)
    out_ref[...] = take(mixed, order).astype(BF16)


def carry_first_kernel(dims, order, ends_ref, inside_ref, *refs):
    add_carried(dims, order, jnp.sum(ends_ref[...] * inside_ref[...], axis=0), *refs)


def carry_second_kernel(dims, order, ends_ref, inside_ref, before_ref, cross_ref, *refs):
    enter = jnp.sum(ends_ref[...] * inside_ref[...], axis=0)
    add_carried(dims, order, enter + before_ref[...] * cross_ref[...], *refs)


def gate_out_kernel(order, query_ref, mixed_ref, out_ref):
    chan, length = out_ref.shape[1], out_ref.shape[0]
    mixed = take(mixed_ref[...], inverse(order)).reshape(chan, length).T
    out_ref[...] = (query_ref[...].astype(F32) * mixed.astype(F32)).astype(BF16)


def on_device(query, keys, values, decay, residue, skip):
    seq_count = lax.axis_size("yc")
    blocks = lax.axis_size("chan")
    length, chan = query.shape
    rows = skip.shape[0]
    groups, modes = decay.shape
    size = rows // groups
    lanes = size * modes
    dims = (blocks, groups, size, length, modes)
    shape = jax.ShapeDtypeStruct
    whole = length * chan

    decay_row = jnp.tile(decay, (1, size))
    residue_row = jnp.tile(residue, (1, size))
    skip_col = skip.reshape(rows, 1)
    place = lax.axis_index("yc").astype(jnp.int32).reshape(1)

    def exchange(axis, order):
        return lambda a: lax.all_to_all(
            a, axis, 0, 0, tiled=True, axis_index_groups=[list(order)]
        )

    gated = call(
        functools.partial(gate_in_kernel, TOKENS_IN), shape((blocks, rows, length), BF16),
        [HBM] * 2, whole, 6 * whole, 60,
        scratch_shapes=[
            pltpu.VMEM((1, length, chan), BF16),
            pltpu.VMEM((1, length, chan), BF16),
            pltpu.SemaphoreType.DMA((1, 2)),
        ],
    )(keys, values)
    z = exchange("chan", TOKENS_IN)(gated)
    table = shape((groups, length, lanes), BF16)
    conv_table = shape((groups, length, length), BF16)
    weights = shape((seq_count, groups, lanes), F32)
    vector = shape((groups, lanes), F32)
    high, low, step, grow, inside, total_w, cross, conv_high, conv_low, after, query_in = call(
        functools.partial(table_kernel, dims, STATES),
        (
            table, table, vector, shape((blocks, groups, size, lanes), F32),
            weights, weights, vector,
            conv_table, conv_table, shape((2, groups, length, lanes), BF16),
            shape((length, chan), BF16),
        ),
        [SMEM, VMEM, VMEM, HBM], 100 * whole, 16 * whole,
        scratch_shapes=[pltpu.SemaphoreType.DMA],
    )(place, decay_row, residue_row, query)
    ends, local = call(
        functools.partial(block_kernel, dims, TOKENS_IN),
        (weights, shape((blocks, groups, size, length), F32)),
        [VMEM] * 8, 8 * length * whole, 16 * whole,
        scratch_shapes=[pltpu.VMEM((blocks, size, lanes), F32)],
    )(z, high, low, step, conv_high, conv_low, after, skip_col)

    half = lax.axis_index("zh")
    ends = lax.cond(half == 0, exchange("yc", STATES), lambda a: a, ends)
    total = call(total_kernel, vector, [VMEM] * 2, whole, whole)(ends, total_w)
    before = lax.ppermute(total, "zh", [(0, 1)])

    def finish(kernel, args):
        mixed = call(
            functools.partial(kernel, dims, TOKENS_OUT), shape((blocks, rows, length), BF16),
            [VMEM] * (len(args) + 3), 12 * lanes * whole, 8 * whole,
        )(*args, grow, after, local)
        return exchange("chan", TOKENS_OUT)(mixed)

    def first_half(ends, mixed):
        return ends, finish(carry_first_kernel, (ends, inside))

    def second_half(ends, mixed):
        return exchange("yc", STATES)(ends), mixed

    def second_finish(mixed, before):
        return finish(carry_second_kernel, (ends, inside, before, cross))

    ends, mixed = lax.cond(half == 0, first_half, second_half, ends, z)
    mixed = lax.cond(half == 1, second_finish, lambda mixed, before: mixed, mixed, before)
    return call(
        functools.partial(gate_out_kernel, TOKENS_OUT), shape((length, chan), BF16),
        [VMEM] * 2, whole, 6 * whole,
    )(query_in, mixed)


def solution(mesh):
    chan = mesh.shape["chan"]
    cut = Mesh(mesh.devices.reshape(HALVES, -1, chan), ("zh", "yc", "chan"))
    tokens = P(("zh", "yc", "chan"), None)
    return jax.shard_map(
        on_device,
        mesh=cut,
        in_specs=(tokens, tokens, tokens, P("chan", None), P("chan", None), P("chan")),
        out_specs=tokens,
        check_vma=False,
    )
```
